256 devices in a mesh: leaf: 64 (over y, z, core), front: 4 (over x).
Axes of the slice: x: 4, y: 4, z: 8, core: 2. Of those that a mesh axis runs over, the one named last changes fastest.
Arguments:
- resid: float32 [262144, 128], P(('leaf', 'front')), may hold values from -6 to 6
- rec_owner: int32 [262144, 1], P(('leaf', 'front')), may hold values from 0 to 63; in each aligned block of 1024 rows (0 to 1023, 1024 to 2047, ...) at most 32 rows name the same one
- rec_cell: int32 [262144], P(('leaf', 'front')), may hold values from 0 to 511
- leaf_inverse: float32 [64, 2, 512, 512], P('leaf', None, 'front'), may hold values from -0.1875 to 0.1875
- couple_up: float32 [64, 3, 2, 1024, 512], P('leaf', None, None, None, 'front'), may hold values from -0.0625 to 0.0625
- sep_inverse: float32 [64, 2, 1024, 1024], P('leaf', None, 'front'), may hold values from -0.125 to 0.125
- couple_down: float32 [64, 3, 2, 512, 1024], P('leaf', None, None, 'front'), may hold values from -0.078125 to 0.078125
- forward_field: float32 [32768, 128], P(('leaf', 'front')), may hold values from -6 to 6
Outputs:
- gradient: float32 [32768], P(('leaf', 'front'))
The draws below stay inside these ranges and needn't reach their ends.
Inputs may be any that keep to these rules, and one draw needn't show every extreme that they name: `rec_owner`: among the receivers of one device at most 32 lie in one subtree, and in every draw some subtree gets exactly 32 from some device.
All inputs are finite; a program needn't handle non-finite values.
Results may differ from the reference program's by a relative error of at most 0.0001.
Values sent between devices are 32-bit elements; how exact they have to be, the bound alone decides.
A program may use at most 64 MiB of HBM per device.

```python
import math
import jax
import jax.numpy as jnp
import numpy as np
from jax import lax

SRC = 64
LC = 512
SEP = 1024
LEVELS = 3
RECV_DEV = 1024
CAP = 32
RECV = 262144
CELLS = 32768
N_LEAF = 64


def place_ends(array, key, smallest, high):
    longest = array.shape.index(max(array.shape))
    spots = []
    for shift in (0, 1):
        where = [jax.random.randint(jax.random.fold_in(key, axis), (), 0, length) for axis, length in enumerate(array.shape)]
        where[longest] = (where[longest] + shift) % array.shape[longest]
        spots.append(tuple(where))
    return array.at[spots[0]].set(smallest).at[spots[1]].set(high)


def block_levels(own_key, dims, pieces, low, top_value):
    def one(axis_at, parts):
        steps = jax.random.uniform(jax.random.fold_in(jax.random.fold_in(own_key, 6), axis_at), (parts,), jnp.float32, low / len(pieces), top_value / len(pieces))
        return jnp.repeat(jnp.exp(steps), dims[axis_at] // parts).reshape((-1,) + (1,) * (len(dims) - axis_at - 1))

    gain = one(*pieces[0])
    for cut in pieces[1:]:
        gain = gain * one(*cut)
    return gain


def shared_out(own_key, own, number, rows, count, top, bound, lean):
    order = jax.random.permutation(own_key, count)
    heavy_load, common = portions_of(count, rows * top, bound, lean, True), portions_of(count, rows * top, bound, lean, False)
    places = jnp.arange(count)

    def named(lengths, turn):
        used = int((lengths > 0).sum())
        fixed = max(1, used // 4)
        shifted = fixed + (places - fixed + turn * (used - fixed)) % max(1, count - fixed)
        return jnp.zeros((count,), jnp.int32).at[order[jnp.where(places < fixed, places, shifted)]].set(jnp.asarray(lengths, jnp.int32))

    lengths = jnp.where(number % 4 == 0, named(heavy_load, number // 4), named(common, number - number // 4 - 1))
    mixed = jax.random.permutation(jax.random.fold_in(own, 3), count)
    source_of, receiver = mixed[0:count // 2 * 2:2], mixed[1:count // 2 * 2:2]
    margin = jnp.minimum(lengths[source_of] - 1, bound - lengths[receiver]) // 2
    margin = jnp.where((source_of == order[0]) | (receiver == order[0]) | (lengths[receiver] == 0), 0, jnp.maximum(margin, 0))
    shifted = jax.random.randint(jax.random.fold_in(own, 4), (count // 2,), 0, 1 << 20) % (margin + 1)
    lengths = lengths.at[source_of].add(-shifted).at[receiver].add(shifted)
    labels = jnp.searchsorted(jnp.cumsum(lengths), jnp.arange(rows * top), side="right").astype(jnp.int32)
    grid = labels.reshape(top, rows).T
    grid = grid[jax.random.permutation(jax.random.fold_in(own, 1), rows)]
    turn = jax.random.randint(jax.random.fold_in(own, 2), (rows, 1), 0, top)
    return jnp.take_along_axis(grid, (jnp.arange(top)[None, :] + turn) % top, axis=1)


def portions_of(count, total, most, slope, full):
    loads = [(1 << 20) // math.isqrt(rank ** slope) + 1 for rank in range(1, count + 1)]
    largest = most if full else min(most, max(-(-total // count), total * loads[0] // sum(loads)))
    least = 1 if total - largest >= count - 1 else 0
    given, rest = [largest] + [least] * (count - 1), total - largest - least * (count - 1)
    while rest > 0:
        free = [i for i in range(1, count) if given[i] < largest] or [i for i in range(1, count) if given[i] < most]
        whole, budget = sum([loads[i] for i in free]), rest
        for i in free:
            extra = min(most - given[i], max(1, budget * loads[i] // whole), rest)
            given[i] = given[i] + extra
            rest = rest - extra
    return np.array(given)


def centred(key, extent, deviation, reach, pieces=(), dtype=jnp.bfloat16):
    level = block_levels(key, extent, pieces, -0.22, 0.18) if pieces else 1.0
    result = jax.random.normal(key, extent, jnp.float32) * deviation * level
    return jnp.minimum(jnp.maximum(result, -reach), reach).astype(dtype)


def setup_inputs(seed: int = 0) -> dict:
    key_list = jax.random.split(jax.random.key(seed), 9)
    resid = centred(key_list[0], (RECV, 2 * SRC), 1.0, 6.0, ((0, 256),), jnp.float32)
    rec_owner_keys = jax.random.split(jax.random.fold_in(key_list[1], 1), RECV // RECV_DEV)
    rec_owner_turns = jax.random.permutation(jax.random.fold_in(key_list[1], 3), RECV // RECV_DEV)
    rec_owner = jax.vmap(lambda own, number: shared_out(jax.random.fold_in(key_list[1], 2), own, number, RECV_DEV, N_LEAF, 1, CAP, 2))(rec_owner_keys, rec_owner_turns).reshape((RECV, 1))
    rec_cell = place_ends(jax.random.randint(key_list[2], (RECV,), 0, LC), jax.random.fold_in(key_list[2], 1), 0, LC - 1).astype(jnp.int32)
    leaf_inverse = centred(key_list[3], (N_LEAF, 2, LC, LC), (2 * LC) ** -0.5, 0.1875, ((0, 64), (2, 4)), jnp.float32)
    couple_up = centred(key_list[4], (N_LEAF, LEVELS, 2, SEP, LC), (2 * LC * 2 ** LEVELS) ** -0.5, 0.0625, ((0, 64), (4, 4)), jnp.float32)
    sep_inverse = centred(key_list[5], (N_LEAF, 2, SEP, SEP), (2 * SEP) ** -0.5, 0.125, ((0, 64), (2, 4)), jnp.float32)
    couple_down = centred(key_list[6], (N_LEAF, LEVELS, 2, LC, SEP), (2 * SEP * LEVELS) ** -0.5, 0.078125, ((0, 64), (3, 4)), jnp.float32)
    forward_field = centred(key_list[7], (CELLS, 2 * SRC), 1.0, 6.0, ((0, 256),), jnp.float32)
    return dict(resid=resid, rec_owner=rec_owner, rec_cell=rec_cell, leaf_inverse=leaf_inverse, couple_up=couple_up, sep_inverse=sep_inverse, couple_down=couple_down, forward_field=forward_field)


def rotate(field):
    half = field.shape[-1] // 2
    return jnp.concatenate([-field[..., half:], field[..., :half]], -1)


def complex_apply(form, mats_real, mats_imag, field):
    first = jnp.einsum(form, mats_real, field, precision=lax.Precision.HIGHEST)
    second = jnp.einsum(form, mats_imag, field, precision=lax.Precision.HIGHEST)
    return first + rotate(second)


def reference(resid, rec_owner, rec_cell, leaf_inverse, couple_up, sep_inverse, couple_down, forward_field):
    columns = 2 * SRC
    targets = (rec_owner[:, 0] * LC + rec_cell).astype(jnp.int32)
    source = jnp.zeros((N_LEAF * LC, columns), jnp.float32).at[targets].add(resid)
    source = source.reshape(N_LEAF, LC, columns)
    forward = complex_apply("nab,nbc->nac", leaf_inverse[:, 0], leaf_inverse[:, 1], source)
    terms = -complex_apply("nksb,nbc->nksc", couple_up[:, :, 0], couple_up[:, :, 1], forward)
    correction = jnp.zeros((N_LEAF, LC, columns), jnp.float32)
    for level in range(1, LEVELS + 1):
        span = 2 ** level
        blocks = N_LEAF // span
        pending = jnp.sum(terms[:, level - 1].reshape(blocks, span, SEP, columns), 1)
        owners = (jnp.arange(blocks) * span + span // 2 - 1).astype(jnp.int32)
        chosen = sep_inverse[owners]
        separator = complex_apply("nab,nbc->nac", chosen[:, 0], chosen[:, 1], pending)
        spread = jnp.repeat(separator, span, axis=0)
        correction = correction + complex_apply("nab,nbc->nac", couple_down[:, level - 1, 0], couple_down[:, level - 1, 1], spread)
    adjoint = (forward - correction).reshape(N_LEAF * LC, columns)
    product = forward_field[:, :SRC] * adjoint[:, :SRC] - forward_field[:, SRC:] * adjoint[:, SRC:]
    return 0.125 * jnp.sum(product, 1)
```

```python
import jax
import jax.numpy as jnp
from jax import lax
from jax.experimental import pallas as pl
from jax.experimental.pallas import tpu as pltpu
from jax.sharding import PartitionSpec as P

F32, BF16, I32 = jnp.float32, jnp.bfloat16, jnp.int32
MESH = pl.DeviceIdType.MESH
DMA = pltpu.SemaphoreType.DMA


def split(value):
    high = value.astype(BF16)
    return high, (value - high.astype(F32)).astype(BF16)


def dot(a, b):
    return jnp.dot(a, b, preferred_element_type=F32)


def rotate(field):
    lane = lax.broadcasted_iota(I32, field.shape, 1)
    turned = pltpu.roll(field, 64, 1)
    return jnp.where(lane < 64, -turned, turned)


def operand(field):
    high, low = split(field)
    turned_high, turned_low = split(rotate(field))
    return jnp.concatenate(
        [jnp.concatenate([high, low], 1), jnp.concatenate([turned_high, turned_low], 1)], 0
    )


def product(high, low, right):
    both = dot(high, right)
    return both[:, :128] + both[:, 128:] + dot(low, right[:, :128])


def wait_bytes(ref, sem):
    pltpu.make_async_copy(ref, ref, sem).wait()


def kernel(
    resid, owner, cell, leaf_inverse, couple_up, sep_inverse, couple_down, field, out,
    resid_v, rows_v, a_f, u_f, s_f, d_f, field_v,
    ah, al, uh, ul, sh, sl, dh, dl,
    send, recv, meta_send, meta_recv, part, part_recv, source,
    t_send, t_recv, t_sum, r1, r2, r3, s1, s2, s3, pend, sep, acc, fwd,
    load_sem, send_sem, recv_sem, meta_ssem, meta_rsem, x_ssem, x_rsem, g_ssem, g_rsem,
    core_ssem, core_rsem, rs_ssem, rs_rsem, p_ssem, p_rsem, z_ssem, b_ssem, f_ssem, b_rsem,
):
    leaf = lax.axis_index("leaf")
    x = lax.axis_index("front")
    c = lax.rem(leaf, 2)
    z = lax.rem(lax.div(leaf, 2), 8)
    y = lax.div(leaf, 16)
    zq, zl = lax.rem(z, 4), lax.rem(z, 2)
    base4, base8 = leaf - lax.rem(leaf, 4), leaf - lax.rem(leaf, 8)
    partner = leaf + 1 - 2 * c

    def remote(src, dst, ssem, rsem, to_leaf, to_front):
        return pltpu.make_async_remote_copy(
            src_ref=src, dst_ref=dst, send_sem=ssem, recv_sem=rsem,
            device_id=(to_leaf, to_front), device_id_type=MESH,
        )

    loads = [
        pltpu.make_async_copy(a, b, load_sem.at[i])
        for i, (a, b) in enumerate(
            [
                (resid, resid_v), (leaf_inverse, a_f), (couple_up, u_f),
                (sep_inverse, s_f), (couple_down, d_f), (field, field_v),
            ]
        )
    ]
    for load in loads:
        load.start()

    barrier = pltpu.get_barrier_semaphore()

    def greet(d, carry):
        pl.semaphore_signal(
            barrier, inc=1, device_id=(lax.rem(leaf + d, 64), x), device_id_type=MESH
        )
        return carry

    lax.fori_loop(1, 64, greet, 0)

    def greet_cube(k, carry):
        for dx in (1, 2, 3):
            pl.semaphore_signal(
                barrier, inc=1, device_id=(base8 + k, lax.rem(x + dx, 4)), device_id_type=MESH
            )
        return carry

    lax.fori_loop(0, 8, greet_cube, 0)

    leaf_ids = lax.broadcasted_iota(I32, (64, 128), 0)
    row_id = lax.broadcasted_iota(I32, (128, 128), 0)
    col_id = lax.broadcasted_iota(I32, (128, 128), 1)
    earlier = jnp.where(row_id < col_id, 1.0, 0.0).astype(BF16)
    lane_base = 32 * lax.rem(leaf, 4)
    count = jnp.zeros((64, 1), F32)
    meta = jnp.zeros((128, 128), F32)
    places = []
    for j in range(8):
        own = owner[j : j + 1, :]
        cells = cell[j : j + 1, :]
        member = jnp.where(own == leaf_ids, 1.0, 0.0)
        before = dot(member.astype(BF16), earlier) + count
        rank = jnp.sum(member * before, 0, keepdims=True).astype(I32)
        count = count + jnp.sum(member, 1, keepdims=True)
        places.append(own * 32 + rank)
        low = jnp.bitwise_and(cells, 31)
        parts = jnp.concatenate(
            [member * (cells - low).astype(F32), member * (low + 1).astype(F32)], 0
        ).astype(BF16)
        spot = jnp.where(rank == row_id - lane_base, 1.0, 0.0).astype(BF16)
        meta = meta + lax.dot_general(
            parts, spot, (((1,), (1,)), ((), ())), preferred_element_type=F32
        )
    meta_send[...] = (meta[:64] + meta[64:]).reshape(64, 1, 128)

    loads[0].wait()
    high, low = split(resid_v[...])
    rows_v[:, :128] = high
    rows_v[:, 128:] = low

    pl.semaphore_wait(barrier, 87)

    slot_ids = lax.broadcasted_iota(I32, (512, 128), 0)
    for dy in (2, 1, 3, 0):
        yd = lax.rem(y + dy, 4)
        slots = slot_ids + yd * 512
        pick = jnp.concatenate(
            [jnp.where(place == slots, 1.0, 0.0).astype(BF16) for place in places], 1
        )
        rows = dot(pick, rows_v[...])
        send[dy] = rows[:, :128] + rows[:, 128:]

        def push(k, carry):
            dz = lax.rem(lax.div(k, 2) * 3 + 4, 8)
            zd, cd = lax.rem(z + dz, 8), lax.rem(c + lax.rem(k, 2), 2)
            at = zd * 2 + cd
            to = yd * 16 + at
            src = send.at[dy, pl.ds(pl.multiple_of(at * 32, 32), 32)]
            dst = recv.at[pl.ds(pl.multiple_of(leaf * 32, 32), 32)]

            def far():
                remote(meta_send.at[to], meta_recv.at[leaf], meta_ssem, meta_rsem.at[y], to, x).start()
                remote(src, dst, send_sem, recv_sem.at[y], to, x).start()

            def near():
                pltpu.make_async_copy(meta_send.at[to], meta_recv.at[leaf], meta_rsem.at[y]).start()
                pltpu.make_async_copy(src, dst, recv_sem.at[y]).start()

            if dy:
                far()
            else:
                pl.when(to != leaf)(far)
                pl.when(to == leaf)(near)
            return carry

        lax.fori_loop(0, 16, push, 0)

    for load in loads[1:]:
        load.wait()
    for m in range(2):
        high, low = split(a_f[m])
        ah[:, m * 512 : m * 512 + 512] = high
        al[:, m * 512 : m * 512 + 512] = low

    def split_up(i, carry):
        level, at = lax.div(i, 8), pl.ds(pl.multiple_of(lax.rem(i, 8) * 128, 128), 128)
        for m in range(2):
            high, low = split(u_f[level, m, at])
            uh[level, at, m * 128 : m * 128 + 128] = high
            ul[level, at, m * 128 : m * 128 + 128] = low
        return carry

    lax.fori_loop(0, 24, split_up, 0)

    def split_sep(i, carry):
        at = pl.ds(pl.multiple_of(i * 32, 32), 32)
        for m in range(2):
            high, low = split(s_f[m, at])
            sh[at, m * 1024 : m * 1024 + 1024] = high
            sl[at, m * 1024 : m * 1024 + 1024] = low
        return carry

    lax.fori_loop(0, 8, split_sep, 0)

    def split_down(i, carry):
        level, at = lax.div(i, 4), pl.ds(pl.multiple_of(lax.rem(i, 4) * 32, 32), 32)
        for m in range(2):
            for f in range(4):
                high, low = split(d_f[level, m, at, f * 256 : f * 256 + 256])
                dh[level, f, at, m * 256 : m * 256 + 256] = high
                dl[level, f, at, m * 256 : m * 256 + 256] = low
        return carry

    lax.fori_loop(0, 12, split_down, 0)

    for step, dy in enumerate((2, 1, 3, 0)):
        ys = lax.rem(y + 4 - dy, 4)
        at = pl.ds(pl.multiple_of(ys * 512, 512), 512)
        wait_bytes(meta_recv.at[pl.ds(ys * 16, 16)], meta_rsem.at[ys])
        wait_bytes(recv.at[at], recv_sem.at[ys])
        hits = []
        for q in range(4):
            row = meta_recv[ys * 16 + q * 4]
            for i in range(1, 4):
                row = row + meta_recv[ys * 16 + q * 4 + i]
            hits.append(jnp.where(row.astype(I32) == slot_ids + 1, 1.0, 0.0).astype(BF16))
        both = dot(jnp.concatenate(hits, 1), jnp.concatenate(split(recv[at]), 1))
        both = both[:, :128] + both[:, 128:]
        if step:
            part[...] += both
        else:
            part[...] = both

    mine = pl.ds(pl.multiple_of(x * 128, 128), 128)
    scatter = [
        remote(
            part.at[pl.ds(pl.multiple_of(lax.rem(x + dx, 4) * 128, 128), 128)],
            part_recv.at[dx - 1], x_ssem.at[dx - 1], x_rsem.at[dx - 1], leaf, lax.rem(x + dx, 4),
        )
        for dx in (1, 2, 3)
    ]
    for copy in (scatter[1], scatter[0], scatter[2]):
        copy.start()
    for copy in scatter:
        copy.wait_recv()
    source[mine] = part[mine] + part_recv[0] + part_recv[1] + part_recv[2]
    gather = [
        remote(
            source.at[mine], source.at[mine], g_ssem.at[dx - 1], g_rsem.at[dx - 1],
            leaf, lax.rem(x + dx, 4),
        )
        for dx in (1, 2, 3)
    ]
    for copy in (gather[1], gather[0], gather[2]):
        copy.start()
    for copy in gather:
        copy.wait_recv()

    forward = product(ah[...], al[...], operand(source[...]))
    fwd[...] = forward
    right = operand(-forward)

    swaps = [
        remote(t_send.at[k], t_recv.at[k], core_ssem.at[k], core_rsem.at[k], partner, x)
        for k in range(3)
    ]
    theirs = pl.ds(pl.multiple_of((1 - c) * 512, 512), 512)
    ours = pl.ds(pl.multiple_of(c * 512, 512), 512)
    for k in (2, 1, 0):
        t_send[k] = product(uh[k, theirs], ul[k, theirs], right)
        swaps[k].start()
    for k in (2, 1, 0):
        t_sum[k] = product(uh[k, ours], ul[k, ours], right)

    stages = ((r1, s1, 1, 128, 0), (r2, s2, 2, 64, zl), (r3, s3, 4, 32, zq))
    for k in (2, 1, 0):
        box, _, span, rows, zk = stages[k]
        swaps[k].wait_recv()
        t_sum[k] += t_recv[k]
        me = zk * 4 + x
        box[me] = t_sum[k, pl.ds(pl.multiple_of(me * rows, rows), rows)]
        for dz in range(span):
            for dx in range(4):
                if dz or dx:
                    zt = lax.rem(zk + dz, span)
                    xt = lax.rem(x + dx, 4)
                    at = pl.ds(pl.multiple_of((zt * 4 + xt) * rows, rows), rows)
                    remote(
                        t_sum.at[k, at], box.at[me], rs_ssem.at[k], rs_rsem.at[k],
                        leaf + 2 * (zt - zk), xt,
                    ).start()

    targets = (leaf - c, base4 + 1, base8 + 3)
    for k in (2, 1, 0):
        box, total, span, rows, zk = stages[k]
        wait_bytes(box.at[pl.ds(0, 4 * span - 1)], rs_rsem.at[k])
        value = box[0]
        for i in range(1, 4 * span):
            value = value + box[i]
        total[...] = value
        at = pl.ds(pl.multiple_of(c * 512 + (zk * 4 + x) * rows, rows), rows)
        for f in range(4):
            local_one = jnp.logical_and(targets[k] == leaf, x == f)

            def far(k=k, f=f, total=total, at=at):
                remote(total, pend.at[at], p_ssem.at[k, f], p_rsem, targets[k], f).start()

            def near(k=k, f=f, total=total, at=at):
                pltpu.make_async_copy(total, pend.at[at], p_rsem).start()

            pl.when(jnp.logical_not(local_one))(far)
            pl.when(local_one)(near)

    owns = lax.rem(leaf, 8) != 7
    level_own = jnp.where(c == 0, 0, jnp.where(zl == 0, 1, 2))

    @pl.when(owns)
    def _():
        wait_bytes(pend, p_rsem)
        sep[level_own, x] = product(sh[...], sl[...], operand(pend[...]))

    def along_x(k):
        for dx in (2, 1, 3):
            xt = lax.rem(x + dx, 4)
            remote(sep.at[k, x], sep.at[k, x], b_ssem.at[k, dx - 1], b_rsem.at[k, x], leaf, xt).start()

    def across(k, f):
        remote(sep.at[k, f], sep.at[k, f], f_ssem.at[k, f], b_rsem.at[k, f], partner, x).start()

    def arrived(k, f):
        wait_bytes(sep.at[k, f], b_rsem.at[k, f])

    def along_z(k, i, to):
        return remote(sep.at[k, x], sep.at[k, x], z_ssem.at[i], b_rsem.at[k, x], to, x)

    z_sends2 = (along_z(1, 0, leaf + 2),)
    z_sends3 = (along_z(2, 0, base8 + 7), along_z(2, 1, base8 + 5), along_z(2, 2, base8 + 1))
    is2 = jnp.logical_and(c == 1, zl == 0)
    is3 = jnp.logical_and(c == 1, zq == 1)

    @pl.when(is2)
    def _():
        for copy in z_sends2:
            copy.start()

    @pl.when(is3)
    def _():
        for copy in z_sends3:
            copy.start()

    @pl.when(c == 0)
    def _():
        along_x(0)
        across(0, x)

    @pl.when(is2)
    def _():
        along_x(1)
        across(1, x)
        arrived(2, x)
        along_x(2)
        across(2, x)

    @pl.when(is3)
    def _():
        along_x(2)
        across(2, x)
        arrived(1, x)
        along_x(1)
        across(1, x)

    @pl.when(jnp.logical_and(c == 1, zq == 3))
    def _():
        for k in (1, 2):
            arrived(k, x)
            along_x(k)
            across(k, x)

    acc[...] = jnp.zeros_like(acc)

    def consume(f):
        for k in range(3):
            acc[...] += product(dh[k, f], dl[k, f], operand(sep[k, f]))

    @pl.when(c == 0)
    def _():
        for k in (1, 2):
            arrived(k, x)

    @pl.when(c == 1)
    def _():
        arrived(0, x)

    last = x
    for dx in (1, 3, 2):
        f = lax.rem(x + dx, 4)

        @pl.when(c == 0)
        def _():
            arrived(0, f)
            across(0, f)

        @pl.when(c == 1)
        def _():
            for k in (1, 2):
                arrived(k, f)
                across(k, f)

        consume(last)

        @pl.when(c == 0)
        def _():
            for k in (1, 2):
                arrived(k, f)

        @pl.when(c == 1)
        def _():
            arrived(0, f)

        last = f
    consume(last)

    weight = jnp.where(col_id < 64, 0.125, -0.125)
    value = field_v[...] * (fwd[...] - acc[...]) * weight
    out[...] = jnp.sum(value.T, 0, keepdims=True)

    wait_bytes(recv.at[pl.ds(0, 63 * 32)], send_sem)
    wait_bytes(meta_recv.at[pl.ds(0, 63)], meta_ssem)
    for copy in scatter + gather + swaps:
        copy.wait_send()
    for k in range(3):
        box, total, span, rows, zk = stages[k]
        wait_bytes(box.at[pl.ds(0, 4 * span - 1)], rs_ssem.at[k])
        for f in range(4):
            local_one = jnp.logical_and(targets[k] == leaf, x == f)

            @pl.when(jnp.logical_not(local_one))
            def _(k=k, f=f, total=total):
                wait_bytes(total, p_ssem.at[k, f])

    @pl.when(is2)
    def _():
        for copy in z_sends2:
            copy.wait_send()

    @pl.when(is3)
    def _():
        for copy in z_sends3:
            copy.wait_send()

    def drain(k):
        for dx in (1, 2, 3):
            wait_bytes(sep.at[k, x], b_ssem.at[k, dx - 1])
        for f in range(4):
            wait_bytes(sep.at[k, f], f_ssem.at[k, f])

    @pl.when(c == 0)
    def _():
        drain(0)

    @pl.when(c == 1)
    def _():
        drain(1)
        drain(2)


def local(
    resid, rec_owner, rec_cell, leaf_inverse, couple_up, sep_inverse, couple_down, forward_field
):
    vmem = pl.BlockSpec(memory_space=pltpu.VMEM)
    hbm = pl.BlockSpec(memory_space=pl.ANY)
    V = pltpu.VMEM
    out = pl.pallas_call(
        kernel,
        out_shape=jax.ShapeDtypeStruct((1, 128), F32),
        in_specs=[hbm, vmem, vmem, hbm, hbm, hbm, hbm, hbm],
        out_specs=vmem,
        scratch_shapes=[
            V((1024, 128), F32), V((1024, 256), BF16),
            V((2, 128, 512), F32), V((3, 2, 1024, 128), F32),
            V((2, 256, 1024), F32), V((3, 2, 128, 1024), F32), V((128, 128), F32),
            V((128, 1024), BF16), V((128, 1024), BF16),
            V((3, 1024, 256), BF16), V((3, 1024, 256), BF16),
            V((256, 2048), BF16), V((256, 2048), BF16),
            V((3, 4, 128, 512), BF16), V((3, 4, 128, 512), BF16),
            V((4, 512, 128), F32), V((2048, 128), F32),
            V((64, 1, 128), F32), V((64, 1, 128), F32),
            V((512, 128), F32), V((3, 128, 128), F32), V((512, 128), F32),
            V((3, 512, 128), F32), V((3, 512, 128), F32), V((3, 512, 128), F32),
            V((4, 128, 128), F32), V((8, 64, 128), F32), V((16, 32, 128), F32),
            V((128, 128), F32), V((64, 128), F32), V((32, 128), F32),
            V((1024, 128), F32), V((3, 4, 256, 128), F32), V((128, 128), F32), V((128, 128), F32),
            DMA((6,)), DMA, DMA((4,)), DMA, DMA((4,)), DMA((3,)), DMA((3,)), DMA((3,)), DMA((3,)),
            DMA((3,)), DMA((3,)), DMA((3,)), DMA((3,)), DMA((3, 4)), DMA,
            DMA((3,)), DMA((3, 3)), DMA((3, 4)), DMA((3, 4)),
        ],
        compiler_params=pltpu.CompilerParams(
            collective_id=0, has_side_effects=True, vmem_limit_bytes=48 * 1024 * 1024
        ),
        name="adjoint_gradient",
    )(
        resid, rec_owner.reshape(8, 128), rec_cell.reshape(8, 128), leaf_inverse[0], couple_up[0],
        sep_inverse[0], couple_down[0], forward_field,
    )
    return out.reshape(128)


def solution(mesh):
    placed = (
        P(("leaf", "front"), None),
        P(("leaf", "front"), None),
        P(("leaf", "front")),
        P("leaf", None, "front", None),
        P("leaf", None, None, None, "front"),
        P("leaf", None, "front", None),
        P("leaf", None, None, "front", None),
        P(("leaf", "front"), None),
    )
    return jax.shard_map(
        local, mesh=mesh, in_specs=placed, out_specs=P(("leaf", "front")), check_vma=False
    )
```

```python
import jax
import jax.numpy as jnp
from jax import lax
from jax.experimental import pallas as pl
from jax.experimental.pallas import tpu as pltpu
from jax.sharding import PartitionSpec as P

F32, BF16, I32 = jnp.float32, jnp.bfloat16, jnp.int32
MESH = pl.DeviceIdType.MESH
DMA = pltpu.SemaphoreType.DMA


def split(value):
    high = value.astype(BF16)
    return high, (value - high.astype(F32)).astype(BF16)


def dot(a, b):
    return jnp.dot(a, b, preferred_element_type=F32)


def dot_rows(a, b):
    return lax.dot_general(a, b, (((1,), (1,)), ((), ())), preferred_element_type=F32)


def rotate(field):
    lane = lax.broadcasted_iota(I32, field.shape, 1)
    turned = pltpu.roll(field, 64, 1)
    return jnp.where(lane < 64, -turned, turned)


def operand(field):
    high, low = split(field)
    turned_high, turned_low = split(rotate(field))
    return jnp.concatenate(
        [jnp.concatenate([high, low], 1), jnp.concatenate([turned_high, turned_low], 1)], 0
    )


def product(high, low, right):
    both = dot(high, right)
    return both[:, :128] + both[:, 128:] + dot(low, right[:, :128])


def wait_bytes(ref, sem):
    pltpu.make_async_copy(ref, ref, sem).wait()


def kernel(
    resid, owner_h, cell_h, leaf_inverse, couple_up, sep_inverse, couple_down, field, out,
    owner, cell, resid_v, rows_v, a_f, u_f, s_f, d_f, field_v,
    ah, al, uh, ul, sh, sl, dh, dl,
    send, recv, meta_send, meta_recv, part, z_recv, source,
    t_send, t_recv, t_sum, r1, r2, r3, s1, s2, s3, pend, sep, acc, fwd,
    load_sem, send_sem, recv_sem, meta_ssem, meta_rsem, zr_ssem, zr_rsem, g_ssem, g_rsem,
    core_ssem, core_rsem, rs_ssem, rs_rsem, p_ssem, p_rsem, z_ssem, b_ssem, f_ssem, b_rsem,
):
    leaf = lax.axis_index("leaf")
    x = lax.axis_index("front")
    c = lax.rem(leaf, 2)
    z = lax.rem(lax.div(leaf, 2), 8)
    y = lax.div(leaf, 16)
    zq, zl = lax.rem(z, 4), lax.rem(z, 2)
    base4, base8 = leaf - lax.rem(leaf, 4), leaf - lax.rem(leaf, 8)
    partner = leaf + 1 - 2 * c

    def remote(src, dst, ssem, rsem, to_leaf, to_front):
        return pltpu.make_async_remote_copy(
            src_ref=src, dst_ref=dst, send_sem=ssem, recv_sem=rsem,
            device_id=(to_leaf, to_front), device_id_type=MESH,
        )

    loads = [
        pltpu.make_async_copy(a, b, load_sem.at[i])
        for i, (a, b) in enumerate(
            [
                (owner_h, owner), (cell_h, cell), (resid, resid_v), (leaf_inverse, a_f), (couple_up, u_f),
                (sep_inverse, s_f), (couple_down, d_f), (field, field_v),
            ]
        )
    ]
    for load in loads:
        load.start()

    barrier = pltpu.get_barrier_semaphore()

    def greet(to_leaf, to_front):
        pl.semaphore_signal(barrier, inc=1, device_id=(to_leaf, to_front), device_id_type=MESH)

    def greet_plane(dy, carry):
        for cd in range(2):
            for dx in (1, 2, 3):
                greet((lax.rem(y + dy, 4) * 8 + z) * 2 + cd, lax.rem(x + dx, 4))
        return carry

    lax.fori_loop(0, 4, greet_plane, 0)

    def greet_column(dy, carry):
        for cd in range(2):
            greet((lax.rem(y + dy, 4) * 8 + z) * 2 + cd, x)
        return carry

    lax.fori_loop(1, 4, greet_column, 0)
    greet(partner, x)

    def greet_z(dz, carry):
        greet((y * 8 + lax.rem(z + dz, 8)) * 2 + c, x)
        return carry

    lax.fori_loop(1, 8, greet_z, 0)

    def greet_cube(dz, carry):
        at = base8 + 2 * lax.rem(zq + dz, 4)
        greet(at + 1 - c, x)
        for cd in range(2):
            for dx in (1, 2, 3):
                greet(at + cd, lax.rem(x + dx, 4))
        return carry

    lax.fori_loop(1, 4, greet_cube, 0)

    loads[0].wait()
    loads[1].wait()
    leaf_ids = lax.broadcasted_iota(I32, (64, 128), 0)
    row_id = lax.broadcasted_iota(I32, (128, 128), 0)
    col_id = lax.broadcasted_iota(I32, (128, 128), 1)
    earlier = jnp.where(row_id < col_id, 1.0, 0.0).astype(BF16)
    count = jnp.zeros((64, 1), F32)
    meta = jnp.zeros((32, 128), F32)
    places = []
    for j in range(8):
        own = owner[j : j + 1, :]
        cells = cell[j : j + 1, :]
        member = jnp.where(own == leaf_ids, 1.0, 0.0)
        before = dot(member.astype(BF16), earlier) + count
        rank = jnp.sum(member * before, 0, keepdims=True).astype(I32)
        count = count + jnp.sum(member, 1, keepdims=True)
        places.append(own * 32 + rank)
        line = jnp.right_shift(own, 4) * 4 + jnp.bitwise_and(own, 1) * 2
        line = line + jnp.bitwise_and(jnp.right_shift(own, 1), 1)
        lane = jnp.bitwise_and(jnp.right_shift(own, 2), 3) * 32 + rank
        on_line = jnp.where(line == leaf_ids[:16], 1.0, 0.0)
        low = jnp.bitwise_and(cells, 31)
        parts = jnp.concatenate(
            [on_line * (cells - low).astype(F32), on_line * (low + 1).astype(F32)], 0
        ).astype(BF16)
        meta = meta + dot_rows(parts, jnp.where(lane == row_id, 1.0, 0.0).astype(BF16))
    meta = meta[:16] + meta[16:]
    for i in range(16):
        meta_send[i // 2, i % 2 : i % 2 + 1, :] = meta[i : i + 1]

    loads[2].wait()
    high, low = split(resid_v[...].T)
    rows_v[:128] = high
    rows_v[128:] = low

    pl.semaphore_wait(barrier, 59)

    slot = lax.broadcasted_iota(I32, (256, 128), 0)
    slot = (
        jnp.bitwise_and(jnp.right_shift(slot, 7), 1) * 32
        + jnp.bitwise_and(jnp.right_shift(slot, 5), 3) * 128
        + jnp.bitwise_and(slot, 31)
    )
    me_plane = y * 8 + x * 2 + c
    for h in range(2):
        for dy in (2, 1, 3, 0):
            yd = lax.rem(y + dy, 4)
            slots = slot + (yd * 512 + h * 64)
            pick = jnp.concatenate(
                [jnp.where(place == slots, 1.0, 0.0).astype(BF16) for place in places], 1
            )
            rows = dot_rows(rows_v[...], pick)
            rows = rows[:128] + rows[128:]
            for cd in range(2):
                send[h, dy, cd] = rows[:, cd * 128 : cd * 128 + 128]

            def push(k, carry):
                xt = lax.rem(x + 2 + lax.div(k, 2), 4)
                cd = lax.rem(c + lax.rem(k, 2), 2)
                to = (yd * 8 + z) * 2 + cd
                src = send.at[h, dy, cd, pl.ds(pl.multiple_of(xt * 32, 32), 32)]
                dst = recv.at[h, me_plane]
                meta_src, meta_dst = meta_send.at[yd * 2 + cd], meta_recv.at[me_plane]

                def far():
                    if h == 0:
                        remote(meta_src, meta_dst, meta_ssem, meta_rsem.at[y], to, xt).start()
                    remote(src, dst, send_sem.at[h], recv_sem.at[h, y], to, xt).start()

                def near():
                    if h == 0:
                        pltpu.make_async_copy(meta_src, meta_dst, meta_rsem.at[y]).start()
                    pltpu.make_async_copy(src, dst, recv_sem.at[h, y]).start()

                if dy:
                    far()
                else:
                    self_copy = jnp.logical_and(to == leaf, xt == x)
                    pl.when(jnp.logical_not(self_copy))(far)
                    pl.when(self_copy)(near)
                return carry

            lax.fori_loop(0, 8, push, 0)

    for load in loads[3:]:
        load.wait()
    for m in range(2):
        high, low = split(a_f[m])
        ah[:, m * 512 : m * 512 + 512] = high
        al[:, m * 512 : m * 512 + 512] = low

    def split_up(i, carry):
        level, at = lax.div(i, 8), pl.ds(pl.multiple_of(lax.rem(i, 8) * 128, 128), 128)
        for m in range(2):
            high, low = split(u_f[level, m, at])
            uh[level, at, m * 128 : m * 128 + 128] = high
            ul[level, at, m * 128 : m * 128 + 128] = low
        return carry

    lax.fori_loop(0, 24, split_up, 0)

    def split_sep(i, carry):
        at = pl.ds(pl.multiple_of(i * 32, 32), 32)
        for m in range(2):
            high, low = split(s_f[m, at])
            sh[at, m * 1024 : m * 1024 + 1024] = high
            sl[at, m * 1024 : m * 1024 + 1024] = low
        return carry

    lax.fori_loop(0, 8, split_sep, 0)

    def split_down(i, carry):
        level, at = lax.div(i, 4), pl.ds(pl.multiple_of(lax.rem(i, 4) * 32, 32), 32)
        for m in range(2):
            for f in range(4):
                high, low = split(d_f[level, m, at, f * 256 : f * 256 + 256])
                dh[level, f, at, m * 256 : m * 256 + 256] = high
                dl[level, f, at, m * 256 : m * 256 + 256] = low
        return carry

    lax.fori_loop(0, 12, split_down, 0)

    cell_ids = lax.broadcasted_iota(I32, (512, 128), 0) + 1
    diagonal = jnp.where(jnp.right_shift(row_id, 5) == jnp.right_shift(col_id, 5), 1.0, 0.0)
    diagonal = diagonal.astype(BF16)
    for h in range(2):
        for step, dy in enumerate((2, 1, 3, 0)):
            ys = lax.rem(y + 4 - dy, 4)
            if h == 0:
                wait_bytes(meta_recv.at[pl.ds(ys * 8, 8)], meta_rsem.at[ys])
            wait_bytes(recv.at[h, pl.ds(ys * 8, 8)], recv_sem.at[h, ys])
            hits, values = [], []
            for i in range(8):
                line = meta_recv[ys * 8 + i][h : h + 1, :].astype(I32)
                hits.append(jnp.where(line == cell_ids, 1.0, 0.0).astype(BF16))
                values.append(
                    jnp.concatenate(
                        [
                            jnp.concatenate([piece] * 4, 0) * diagonal
                            for piece in split(recv[h, ys * 8 + i])
                        ],
                        0,
                    )
                )
            both = dot_rows(jnp.concatenate(values, 1), jnp.concatenate(hits, 1))
            both = both[:128] + both[128:]
            if step:
                part[h] += both
            else:
                part[h] = both
        for i in (2, 1, 3, 0):
            zd = lax.rem(z + lax.rem(z + h, 2) + 2 * i, 8)
            to = (y * 8 + zd) * 2 + c
            src = part.at[h, pl.ds(pl.multiple_of(lax.div(zd, 2) * 32, 32), 32)]

            def far(src=src, to=to):
                remote(src, z_recv.at[z], zr_ssem, zr_rsem, to, x).start()

            def near(src=src):
                pltpu.make_async_copy(src, z_recv.at[z], zr_rsem).start()

            pl.when(to != leaf)(far)
            pl.when(to == leaf)(near)

    mine = pl.ds(pl.multiple_of(x * 32, 32), 32)
    wait_bytes(z_recv, zr_rsem)
    total = z_recv[0]
    for i in range(1, 8):
        total = total + z_recv[i]
    source[mine] = total
    gather = [
        remote(
            source.at[mine], source.at[mine], g_ssem.at[dx - 1], g_rsem.at[dx - 1],
            leaf, lax.rem(x + dx, 4),
        )
        for dx in (1, 2, 3)
    ]
    for copy in (gather[1], gather[0], gather[2]):
        copy.start()
    for copy in gather:
        copy.wait_recv()

    high, low = split(source[...])
    right = jnp.concatenate(
        [jnp.concatenate([p, jnp.concatenate([-p[64:], p[:64]], 0)], 1) for p in (high, low)], 0
    )
    both = dot_rows(ah[...], right)
    forward = both[:, :128] + both[:, 128:] + dot_rows(al[...], right[:128])
    fwd[...] = forward
    right = operand(-forward)

    swaps = [
        remote(t_send.at[k], t_recv.at[k], core_ssem.at[k], core_rsem.at[k], partner, x)
        for k in range(3)
    ]
    theirs = pl.ds(pl.multiple_of((1 - c) * 512, 512), 512)
    ours = pl.ds(pl.multiple_of(c * 512, 512), 512)
    for k in (2, 1, 0):
        t_send[k] = product(uh[k, theirs], ul[k, theirs], right)
        swaps[k].start()
    for k in (2, 1, 0):
        t_sum[k] = product(uh[k, ours], ul[k, ours], right)

    stages = ((r1, s1, 1, 128, 0), (r2, s2, 2, 64, zl), (r3, s3, 4, 32, zq))
    for k in (2, 1, 0):
        box, _, span, rows, zk = stages[k]
        swaps[k].wait_recv()
        t_sum[k] += t_recv[k]
        me = zk * 4 + x
        box[me] = t_sum[k, pl.ds(pl.multiple_of(me * rows, rows), rows)]
        for dz in range(span):
            for dx in range(4):
                if dz or dx:
                    zt = lax.rem(zk + dz, span)
                    xt = lax.rem(x + dx, 4)
                    at = pl.ds(pl.multiple_of((zt * 4 + xt) * rows, rows), rows)
                    remote(
                        t_sum.at[k, at], box.at[me], rs_ssem.at[k], rs_rsem.at[k],
                        leaf + 2 * (zt - zk), xt,
                    ).start()

    targets = (leaf - c, base4 + 1, base8 + 3)
    for k in (2, 1, 0):
        box, total, span, rows, zk = stages[k]
        wait_bytes(box.at[pl.ds(0, 4 * span - 1)], rs_rsem.at[k])
        value = box[0]
        for i in range(1, 4 * span):
            value = value + box[i]
        total[...] = value
        at = pl.ds(pl.multiple_of(c * 512 + (zk * 4 + x) * rows, rows), rows)
        for f in range(4):
            local_one = jnp.logical_and(targets[k] == leaf, x == f)

            def far(k=k, f=f, total=total, at=at):
                remote(total, pend.at[at], p_ssem.at[k, f], p_rsem, targets[k], f).start()

            def near(k=k, f=f, total=total, at=at):
                pltpu.make_async_copy(total, pend.at[at], p_rsem).start()

            pl.when(jnp.logical_not(local_one))(far)
            pl.when(local_one)(near)

    owns = lax.rem(leaf, 8) != 7
    level_own = jnp.where(c == 0, 0, jnp.where(zl == 0, 1, 2))

    @pl.when(owns)
    def _():
        wait_bytes(pend, p_rsem)
        sep[level_own, x] = product(sh[...], sl[...], operand(pend[...]))

    def along_x(k):
        for dx in (2, 1, 3):
            xt = lax.rem(x + dx, 4)
            remote(sep.at[k, x], sep.at[k, x], b_ssem.at[k, dx - 1], b_rsem.at[k, x], leaf, xt).start()

    def across(k, f):
        remote(sep.at[k, f], sep.at[k, f], f_ssem.at[k, f], b_rsem.at[k, f], partner, x).start()

    def arrived(k, f):
        wait_bytes(sep.at[k, f], b_rsem.at[k, f])

    def along_z(k, i, to):
        return remote(sep.at[k, x], sep.at[k, x], z_ssem.at[i], b_rsem.at[k, x], to, x)

    z_sends2 = (along_z(1, 0, leaf + 2),)
    z_sends3 = (along_z(2, 0, base8 + 7), along_z(2, 1, base8 + 5), along_z(2, 2, base8 + 1))
    is2 = jnp.logical_and(c == 1, zl == 0)
    is3 = jnp.logical_and(c == 1, zq == 1)

    @pl.when(is2)
    def _():
        for copy in z_sends2:
            copy.start()

    @pl.when(is3)
    def _():
        for copy in z_sends3:
            copy.start()

    @pl.when(c == 0)
    def _():
        along_x(0)
        across(0, x)

    @pl.when(is2)
    def _():
        along_x(1)
        across(1, x)
        arrived(2, x)
        along_x(2)
        across(2, x)

    @pl.when(is3)
    def _():
        along_x(2)
        across(2, x)
        arrived(1, x)
        along_x(1)
        across(1, x)

    @pl.when(jnp.logical_and(c == 1, zq == 3))
    def _():
        for k in (1, 2):
            arrived(k, x)
            along_x(k)
            across(k, x)

    acc[...] = jnp.zeros_like(acc)

    def consume(f):
        for k in range(3):
            acc[...] += product(dh[k, f], dl[k, f], operand(sep[k, f]))

    @pl.when(c == 0)
    def _():
        for k in (1, 2):
            arrived(k, x)

    @pl.when(c == 1)
    def _():
        arrived(0, x)

    last = x
    for dx in (1, 3, 2):
        f = lax.rem(x + dx, 4)

        @pl.when(c == 0)
        def _():
            arrived(0, f)
            across(0, f)

        @pl.when(c == 1)
        def _():
            for k in (1, 2):
                arrived(k, f)
                across(k, f)

        consume(last)

        @pl.when(c == 0)
        def _():
            for k in (1, 2):
                arrived(k, f)

        @pl.when(c == 1)
        def _():
            arrived(0, f)

        last = f
    consume(last)

    weight = jnp.where(col_id < 64, 0.125, -0.125)
    value = field_v[...] * (fwd[...] - acc[...]) * weight
    out[...] = jnp.sum(value.T, 0, keepdims=True)

    for h in range(2):
        wait_bytes(recv.at[h, pl.ds(0, 31)], send_sem.at[h])
    wait_bytes(meta_recv.at[pl.ds(0, 31)], meta_ssem)
    wait_bytes(z_recv.at[pl.ds(0, 7)], zr_ssem)
    for copy in gather + swaps:
        copy.wait_send()
    for k in range(3):
        box, total, span, rows, zk = stages[k]
        wait_bytes(box.at[pl.ds(0, 4 * span - 1)], rs_ssem.at[k])
        for f in range(4):
            local_one = jnp.logical_and(targets[k] == leaf, x == f)

            @pl.when(jnp.logical_not(local_one))
            def _(k=k, f=f, total=total):
                wait_bytes(total, p_ssem.at[k, f])

    @pl.when(is2)
    def _():
        for copy in z_sends2:
            copy.wait_send()

    @pl.when(is3)
    def _():
        for copy in z_sends3:
            copy.wait_send()

    def drain(k):
        for dx in (1, 2, 3):
            wait_bytes(sep.at[k, x], b_ssem.at[k, dx - 1])
        for f in range(4):
            wait_bytes(sep.at[k, f], f_ssem.at[k, f])

    @pl.when(c == 0)
    def _():
        drain(0)

    @pl.when(c == 1)
    def _():
        drain(1)
        drain(2)


def local(
    resid, rec_owner, rec_cell, leaf_inverse, couple_up, sep_inverse, couple_down, forward_field
):
    vmem = pl.BlockSpec(memory_space=pltpu.VMEM)
    hbm = pl.BlockSpec(memory_space=pl.ANY)
    V = pltpu.VMEM
    out = pl.pallas_call(
        kernel,
        out_shape=jax.ShapeDtypeStruct((1, 128), F32),
        in_specs=[hbm] * 8,
        out_specs=vmem,
        scratch_shapes=[
            V((8, 128), I32), V((8, 128), I32), V((1024, 128), F32), V((256, 1024), BF16),
            V((2, 128, 512), F32), V((3, 2, 1024, 128), F32),
            V((2, 256, 1024), F32), V((3, 2, 128, 1024), F32), V((128, 128), F32),
            V((128, 1024), BF16), V((128, 1024), BF16),
            V((3, 1024, 256), BF16), V((3, 1024, 256), BF16),
            V((256, 2048), BF16), V((256, 2048), BF16),
            V((3, 4, 128, 512), BF16), V((3, 4, 128, 512), BF16),
            V((2, 4, 2, 128, 128), F32), V((2, 32, 32, 128), F32),
            V((8, 2, 128), F32), V((32, 2, 128), F32),
            V((2, 128, 512), F32), V((8, 32, 512), F32), V((128, 512), F32),
            V((3, 512, 128), F32), V((3, 512, 128), F32), V((3, 512, 128), F32),
            V((4, 128, 128), F32), V((8, 64, 128), F32), V((16, 32, 128), F32),
            V((128, 128), F32), V((64, 128), F32), V((32, 128), F32),
            V((1024, 128), F32), V((3, 4, 256, 128), F32), V((128, 128), F32), V((128, 128), F32),
            DMA((8,)), DMA((2,)), DMA((2, 4)), DMA, DMA((4,)), DMA, DMA, DMA((3,)), DMA((3,)),
            DMA((3,)), DMA((3,)), DMA((3,)), DMA((3,)), DMA((3, 4)), DMA,
            DMA((3,)), DMA((3, 3)), DMA((3, 4)), DMA((3, 4)),
        ],
        compiler_params=pltpu.CompilerParams(
            collective_id=0, has_side_effects=True, vmem_limit_bytes=62 * 1024 * 1024
        ),
        name="adjoint_gradient",
    )(
        resid, rec_owner.reshape(8, 128), rec_cell.reshape(8, 128), leaf_inverse[0], couple_up[0],
        sep_inverse[0], couple_down[0], forward_field,
    )
    return out.reshape(128)


def solution(mesh):
    placed = (
        P(("leaf", "front"), None),
        P(("leaf", "front"), None),
        P(("leaf", "front")),
        P("leaf", None, "front", None),
        P("leaf", None, None, None, "front"),
        P("leaf", None, "front", None),
        P("leaf", None, None, "front", None),
        P(("leaf", "front"), None),
    )
    return jax.shard_map(
        local, mesh=mesh, in_specs=placed, out_specs=P(("leaf", "front")), check_vma=False
    )
```

```python
import jax
import jax.numpy as jnp
from jax import lax
from jax.experimental import pallas as pl
from jax.experimental.pallas import tpu as pltpu
from jax.sharding import PartitionSpec as P

F32, BF16, I32 = jnp.float32, jnp.bfloat16, jnp.int32
MESH = pl.DeviceIdType.MESH
DMA = pltpu.SemaphoreType.DMA


def split(value):
    high = value.astype(BF16)
    return high, (value - high.astype(F32)).astype(BF16)


def dot(a, b):
    return jnp.dot(a, b, preferred_element_type=F32)


def dot_rows(a, b):
    return lax.dot_general(a, b, (((1,), (1,)), ((), ())), preferred_element_type=F32)


def rotate(field):
    lane = lax.broadcasted_iota(I32, field.shape, 1)
    turned = pltpu.roll(field, 64, 1)
    return jnp.where(lane < 64, -turned, turned)


def operand(field):
    high, low = split(field)
    turned_high, turned_low = split(rotate(field))
    return jnp.concatenate(
        [jnp.concatenate([high, low], 1), jnp.concatenate([turned_high, turned_low], 1)], 0
    )


def product(high, low, right):
    both = dot(high, right)
    return both[:, :128] + both[:, 128:] + dot(low, right[:, :128])


def wait_bytes(ref, sem):
    pltpu.make_async_copy(ref, ref, sem).wait()


def kernel(
    resid, owner_h, cell_h, leaf_inverse, couple_up, sep_inverse, couple_down, field, out,
    owner, cell, resid_v, rows_v, a_f, u_f, s_f, d_f, field_v,
    ah, al, uh, ul, sh, sl, dh, dl,
    send, recv, meta_send, meta_recv, part, z_recv, source,
    t_send, t_recv, t_sum, r1, r2, r3, s1, s2, s3, pend, sep, acc, fwd,
    load_sem, send_sem, recv_sem, meta_ssem, meta_rsem, zr_ssem, zr_rsem, g_ssem, g_rsem,
    core_ssem, core_rsem, rs_ssem, rs_rsem, p_ssem, p_rsem, z_ssem, b_ssem, f_ssem, b_rsem,
):
    leaf = lax.axis_index("leaf")
    x = lax.axis_index("front")
    c = lax.rem(leaf, 2)
    z = lax.rem(lax.div(leaf, 2), 8)
    y = lax.div(leaf, 16)
    zq, zl = lax.rem(z, 4), lax.rem(z, 2)
    base4, base8 = leaf - lax.rem(leaf, 4), leaf - lax.rem(leaf, 8)
    partner = leaf + 1 - 2 * c

    def remote(src, dst, ssem, rsem, to_leaf, to_front):
        return pltpu.make_async_remote_copy(
            src_ref=src, dst_ref=dst, send_sem=ssem, recv_sem=rsem,
            device_id=(to_leaf, to_front), device_id_type=MESH,
        )

    loads = [
        pltpu.make_async_copy(a, b, load_sem.at[i])
        for i, (a, b) in enumerate(
            [
                (owner_h, owner), (cell_h, cell), (resid, resid_v), (leaf_inverse, a_f), (couple_up, u_f),
                (sep_inverse, s_f), (couple_down, d_f), (field, field_v),
            ]
        )
    ]
    for load in loads:
        load.start()

    barrier = pltpu.get_barrier_semaphore()

    def greet(to_leaf, to_front):
        pl.semaphore_signal(barrier, inc=1, device_id=(to_leaf, to_front), device_id_type=MESH)

    def greet_plane(dy, carry):
        for cd in range(2):
            for dx in (1, 2, 3):
                greet((lax.rem(y + dy, 4) * 8 + z) * 2 + cd, lax.rem(x + dx, 4))
        return carry

    lax.fori_loop(0, 4, greet_plane, 0)

    def greet_column(dy, carry):
        for cd in range(2):
            greet((lax.rem(y + dy, 4) * 8 + z) * 2 + cd, x)
        return carry

    lax.fori_loop(1, 4, greet_column, 0)
    greet(partner, x)

    def greet_column_z(dz, carry):
        greet((y * 8 + lax.rem(z + 2 * dz, 8)) * 2 + c, x)
        return carry

    lax.fori_loop(1, 4, greet_column_z, 0)

    def greet_neighbour(k, carry):
        for dx in range(4):
            greet(lax.rem(k, 4) * 16 + lax.rem(z + 7 + 2 * c, 8) * 2 + lax.div(k, 4), lax.rem(x + dx, 4))
        return carry

    lax.fori_loop(0, 8, greet_neighbour, 0)

    def greet_cube(dz, carry):
        at = base8 + 2 * lax.rem(zq + dz, 4)
        for dx in range(4):
            greet(at + c, lax.rem(x + dx, 4))

            @pl.when(jnp.logical_and(c == 1, jnp.logical_or(zq == 1, jnp.logical_and(zl == 0, dz == 1))))
            def _():
                greet(at, lax.rem(x + dx, 4))

        return carry

    lax.fori_loop(1, 4, greet_cube, 0)

    loads[0].wait()
    loads[1].wait()
    leaf_ids = lax.broadcasted_iota(I32, (64, 128), 0)
    row_id = lax.broadcasted_iota(I32, (128, 128), 0)
    col_id = lax.broadcasted_iota(I32, (128, 128), 1)
    earlier = jnp.where(row_id < col_id, 1.0, 0.0).astype(BF16)
    count = jnp.zeros((64, 1), F32)
    meta = jnp.zeros((32, 128), F32)
    places = []
    for j in range(8):
        own = owner[j : j + 1, :]
        cells = cell[j : j + 1, :]
        member = jnp.where(own == leaf_ids, 1.0, 0.0)
        before = dot(member.astype(BF16), earlier) + count
        rank = jnp.sum(member * before, 0, keepdims=True).astype(I32)
        count = count + jnp.sum(member, 1, keepdims=True)
        places.append(own * 32 + rank)
        line = jnp.right_shift(own, 4) * 4 + jnp.bitwise_and(own, 1) * 2
        line = line + jnp.bitwise_and(jnp.right_shift(own, 1), 1)
        lane = jnp.bitwise_and(jnp.right_shift(own, 2), 3) * 32 + rank
        on_line = jnp.where(line == leaf_ids[:16], 1.0, 0.0)
        low = jnp.bitwise_and(cells, 31)
        parts = jnp.concatenate(
            [on_line * (cells - low).astype(F32), on_line * (low + 1).astype(F32)], 0
        ).astype(BF16)
        meta = meta + dot_rows(parts, jnp.where(lane == row_id, 1.0, 0.0).astype(BF16))
    meta = meta[:16] + meta[16:]
    for i in range(16):
        meta_send[i] = meta[i : i + 1]

    loads[2].wait()
    high, low = split(resid_v[...].T)
    rows_v[:128] = high
    rows_v[128:] = low

    greetings = 31 + 3 + 32 + 12 + (1 - c) * (4 * zl + jnp.where(zq == 1, 0, 4))
    pl.semaphore_wait(barrier, greetings)

    slot = lax.broadcasted_iota(I32, (256, 128), 0)
    slot = (
        jnp.bitwise_and(jnp.right_shift(slot, 7), 1) * 32
        + jnp.bitwise_and(jnp.right_shift(slot, 5), 3) * 128
        + jnp.bitwise_and(slot, 31)
    )
    me_plane = y * 8 + x * 2 + c
    for h in (1, 0):
        parity = lax.rem(z + h, 2)
        for dy in (2, 1, 3, 0):
            yd = lax.rem(y + dy, 4)
            slots = slot + (yd * 512 + parity * 64)
            pick = jnp.concatenate(
                [jnp.where(place == slots, 1.0, 0.0).astype(BF16) for place in places], 1
            )
            rows = dot_rows(rows_v[...], pick)
            rows = rows[:128] + rows[128:]
            for cd in range(2):
                send[h, dy, cd] = rows[:, cd * 128 : cd * 128 + 128]

            def push(k, carry):
                xt = lax.rem(x + 2 + lax.div(k, 2), 4)
                cd = lax.rem(c + lax.rem(k, 2), 2)
                zt = lax.rem(z + 1 + 6 * cd, 8) if h else z
                to = (yd * 8 + zt) * 2 + cd
                src = send.at[h, dy, cd, pl.ds(pl.multiple_of(xt * 32, 32), 32)]
                dst = recv.at[h, me_plane]
                meta_src = meta_send.at[yd * 4 + cd * 2 + parity]
                meta_dst = meta_recv.at[h, me_plane]

                def far():
                    remote(meta_src, meta_dst, meta_ssem.at[h], meta_rsem.at[h, y], to, xt).start()
                    remote(src, dst, send_sem.at[h], recv_sem.at[h, y], to, xt).start()

                def near():
                    pltpu.make_async_copy(meta_src, meta_dst, meta_rsem.at[h, y]).start()
                    pltpu.make_async_copy(src, dst, recv_sem.at[h, y]).start()

                if dy or h:
                    far()
                else:
                    self_copy = jnp.logical_and(to == leaf, xt == x)
                    pl.when(jnp.logical_not(self_copy))(far)
                    pl.when(self_copy)(near)
                return carry

            lax.fori_loop(0, 8, push, 0)

    for load in loads[3:]:
        load.wait()
    for m in range(2):
        high, low = split(a_f[m])
        ah[:, m * 512 : m * 512 + 512] = high
        al[:, m * 512 : m * 512 + 512] = low

    def split_up(i, carry):
        level, at = lax.div(i, 8), pl.ds(pl.multiple_of(lax.rem(i, 8) * 128, 128), 128)
        for m in range(2):
            high, low = split(u_f[level, m, at])
            uh[level, at, m * 128 : m * 128 + 128] = high
            ul[level, at, m * 128 : m * 128 + 128] = low
        return carry

    lax.fori_loop(0, 24, split_up, 0)

    def split_sep(i, carry):
        at = pl.ds(pl.multiple_of(i * 32, 32), 32)
        for m in range(2):
            high, low = split(s_f[m, at])
            sh[at, m * 1024 : m * 1024 + 1024] = high
            sl[at, m * 1024 : m * 1024 + 1024] = low
        return carry

    lax.fori_loop(0, 8, split_sep, 0)

    def split_down(i, carry):
        level, at = lax.div(i, 4), pl.ds(pl.multiple_of(lax.rem(i, 4) * 32, 32), 32)
        for m in range(2):
            for f in range(4):
                high, low = split(d_f[level, m, at, f * 256 : f * 256 + 256])
                dh[level, f, at, m * 256 : m * 256 + 256] = high
                dl[level, f, at, m * 256 : m * 256 + 256] = low
        return carry

    lax.fori_loop(0, 12, split_down, 0)

    cell_ids = lax.broadcasted_iota(I32, (512, 128), 0) + 1
    diagonal = jnp.where(jnp.right_shift(row_id, 5) == jnp.right_shift(col_id, 5), 1.0, 0.0)
    diagonal = diagonal.astype(BF16)
    for h in (1, 0):
        for dy in (2, 1, 3, 0):
            ys = lax.rem(y + 4 - dy, 4)
            wait_bytes(meta_recv.at[h, pl.ds(ys * 8, 8)], meta_rsem.at[h, ys])
            wait_bytes(recv.at[h, pl.ds(ys * 8, 8)], recv_sem.at[h, ys])
            hits, values = [], []
            for i in range(8):
                line = meta_recv[h, ys * 8 + i].astype(I32)
                hits.append(jnp.where(line == cell_ids, 1.0, 0.0).astype(BF16))
                values.append(
                    jnp.concatenate(
                        [
                            jnp.concatenate([piece] * 4, 0) * diagonal
                            for piece in split(recv[h, ys * 8 + i])
                        ],
                        0,
                    )
                )
            both = dot_rows(jnp.concatenate(values, 1), jnp.concatenate(hits, 1))
            both = both[:128] + both[128:]
            if h and dy == 2:
                part[...] = both
            else:
                part[...] += both

    zh = lax.div(z, 2)
    for i in (2, 1, 3, 0):
        zd = lax.rem(z + 2 * i, 8)
        src = part.at[pl.ds(pl.multiple_of(lax.div(zd, 2) * 32, 32), 32)]
        if i:
            remote(src, z_recv.at[zh], zr_ssem, zr_rsem, (y * 8 + zd) * 2 + c, x).start()
        else:
            pltpu.make_async_copy(src, z_recv.at[zh], zr_rsem).start()

    mine = pl.ds(pl.multiple_of(x * 32, 32), 32)
    wait_bytes(z_recv, zr_rsem)
    total = z_recv[0]
    for i in range(1, 4):
        total = total + z_recv[i]
    source[mine] = total
    gather = [
        remote(
            source.at[mine], source.at[mine], g_ssem.at[dx - 1], g_rsem.at[dx - 1],
            leaf, lax.rem(x + dx, 4),
        )
        for dx in (1, 2, 3)
    ]
    for copy in (gather[1], gather[0], gather[2]):
        copy.start()
    for copy in gather:
        copy.wait_recv()

    high, low = split(source[...])
    right = jnp.concatenate(
        [jnp.concatenate([p, jnp.concatenate([-p[64:], p[:64]], 0)], 1) for p in (high, low)], 0
    )
    both = dot_rows(ah[...], right)
    forward = both[:, :128] + both[:, 128:] + dot_rows(al[...], right[:128])
    fwd[...] = forward
    right = operand(-forward)

    swaps = [
        remote(t_send.at[k], t_recv.at[k], core_ssem.at[k], core_rsem.at[k], partner, x)
        for k in range(3)
    ]
    theirs = pl.ds(pl.multiple_of((1 - c) * 512, 512), 512)
    ours = pl.ds(pl.multiple_of(c * 512, 512), 512)
    for k in (2, 1, 0):
        t_send[k] = product(uh[k, theirs], ul[k, theirs], right)
        swaps[k].start()
    for k in (2, 1, 0):
        t_sum[k] = product(uh[k, ours], ul[k, ours], right)

    stages = ((r1, s1, 1, 128, 0), (r2, s2, 2, 64, zl), (r3, s3, 4, 32, zq))
    for k in (2, 1, 0):
        box, _, span, rows, zk = stages[k]
        swaps[k].wait_recv()
        t_sum[k] += t_recv[k]
        me = zk * 4 + x
        box[me] = t_sum[k, pl.ds(pl.multiple_of(me * rows, rows), rows)]
        for dz in range(span):
            for dx in range(4):
                if dz or dx:
                    zt = lax.rem(zk + dz, span)
                    xt = lax.rem(x + dx, 4)
                    at = pl.ds(pl.multiple_of((zt * 4 + xt) * rows, rows), rows)
                    remote(
                        t_sum.at[k, at], box.at[me], rs_ssem.at[k], rs_rsem.at[k],
                        leaf + 2 * (zt - zk), xt,
                    ).start()

    targets = (leaf - c, base4 + 1, base8 + 3)
    for k in (2, 1, 0):
        box, total, span, rows, zk = stages[k]
        wait_bytes(box.at[pl.ds(0, 4 * span - 1)], rs_rsem.at[k])
        value = box[0]
        for i in range(1, 4 * span):
            value = value + box[i]
        total[...] = value
        at = pl.ds(pl.multiple_of(c * 512 + (zk * 4 + x) * rows, rows), rows)
        for f in range(4):
            local_one = jnp.logical_and(targets[k] == leaf, x == f)

            def far(k=k, f=f, total=total, at=at):
                remote(total, pend.at[at], p_ssem.at[k, f], p_rsem, targets[k], f).start()

            def near(k=k, f=f, total=total, at=at):
                pltpu.make_async_copy(total, pend.at[at], p_rsem).start()

            pl.when(jnp.logical_not(local_one))(far)
            pl.when(local_one)(near)

    owns = lax.rem(leaf, 8) != 7
    level_own = jnp.where(c == 0, 0, jnp.where(zl == 0, 1, 2))

    @pl.when(owns)
    def _():
        wait_bytes(pend, p_rsem)
        sep[level_own, x] = product(sh[...], sl[...], operand(pend[...]))

    def along_x(k):
        for dx in (2, 1, 3):
            xt = lax.rem(x + dx, 4)
            remote(sep.at[k, x], sep.at[k, x], b_ssem.at[k, dx - 1], b_rsem.at[k, x], leaf, xt).start()

    def across(k, f):
        remote(sep.at[k, f], sep.at[k, f], f_ssem.at[k, f], b_rsem.at[k, f], partner, x).start()

    def arrived(k, f):
        wait_bytes(sep.at[k, f], b_rsem.at[k, f])

    def along_z(k, i, to):
        return remote(sep.at[k, x], sep.at[k, x], z_ssem.at[i], b_rsem.at[k, x], to, x)

    z_sends2 = (along_z(1, 0, leaf + 2),)
    z_sends3 = (along_z(2, 0, base8 + 7), along_z(2, 1, base8 + 5), along_z(2, 2, base8 + 1))
    is2 = jnp.logical_and(c == 1, zl == 0)
    is3 = jnp.logical_and(c == 1, zq == 1)

    @pl.when(is2)
    def _():
        for copy in z_sends2:
            copy.start()

    @pl.when(is3)
    def _():
        for copy in z_sends3:
            copy.start()

    @pl.when(c == 0)
    def _():
        along_x(0)
        across(0, x)

    @pl.when(is2)
    def _():
        along_x(1)
        across(1, x)
        arrived(2, x)
        along_x(2)
        across(2, x)

    @pl.when(is3)
    def _():
        along_x(2)
        across(2, x)
        arrived(1, x)
        along_x(1)
        across(1, x)

    @pl.when(jnp.logical_and(c == 1, zq == 3))
    def _():
        for k in (1, 2):
            arrived(k, x)
            along_x(k)
            across(k, x)

    acc[...] = jnp.zeros_like(acc)

    def consume(f):
        for k in range(3):
            acc[...] += product(dh[k, f], dl[k, f], operand(sep[k, f]))

    @pl.when(c == 0)
    def _():
        for k in (1, 2):
            arrived(k, x)

    @pl.when(c == 1)
    def _():
        arrived(0, x)

    last = x
    for dx in (1, 3, 2):
        f = lax.rem(x + dx, 4)

        @pl.when(c == 0)
        def _():
            arrived(0, f)
            across(0, f)

        @pl.when(c == 1)
        def _():
            for k in (1, 2):
                arrived(k, f)
                across(k, f)

        consume(last)

        @pl.when(c == 0)
        def _():
            for k in (1, 2):
                arrived(k, f)

        @pl.when(c == 1)
        def _():
            arrived(0, f)

        last = f
    consume(last)

    weight = jnp.where(col_id < 64, 0.125, -0.125)
    value = field_v[...] * (fwd[...] - acc[...]) * weight
    out[...] = jnp.sum(value.T, 0, keepdims=True)

    for h in range(2):
        wait_bytes(recv.at[h, pl.ds(0, 31 + h)], send_sem.at[h])
        wait_bytes(meta_recv.at[h, pl.ds(0, 31 + h)], meta_ssem.at[h])
    wait_bytes(z_recv.at[pl.ds(0, 3)], zr_ssem)
    for copy in gather + swaps:
        copy.wait_send()
    for k in range(3):
        box, total, span, rows, zk = stages[k]
        wait_bytes(box.at[pl.ds(0, 4 * span - 1)], rs_ssem.at[k])
        for f in range(4):
            local_one = jnp.logical_and(targets[k] == leaf, x == f)

            @pl.when(jnp.logical_not(local_one))
            def _(k=k, f=f, total=total):
                wait_bytes(total, p_ssem.at[k, f])

    @pl.when(is2)
    def _():
        for copy in z_sends2:
            copy.wait_send()

    @pl.when(is3)
    def _():
        for copy in z_sends3:
            copy.wait_send()

    def drain(k):
        for dx in (1, 2, 3):
            wait_bytes(sep.at[k, x], b_ssem.at[k, dx - 1])
        for f in range(4):
            wait_bytes(sep.at[k, f], f_ssem.at[k, f])

    @pl.when(c == 0)
    def _():
        drain(0)

    @pl.when(c == 1)
    def _():
        drain(1)
        drain(2)


def local(
    resid, rec_owner, rec_cell, leaf_inverse, couple_up, sep_inverse, couple_down, forward_field
):
    vmem = pl.BlockSpec(memory_space=pltpu.VMEM)
    hbm = pl.BlockSpec(memory_space=pl.ANY)
    V = pltpu.VMEM
    out = pl.pallas_call(
        kernel,
        out_shape=jax.ShapeDtypeStruct((1, 128), F32),
        in_specs=[hbm] * 8,
        out_specs=vmem,
        scratch_shapes=[
            V((8, 128), I32), V((8, 128), I32), V((1024, 128), F32), V((256, 1024), BF16),
            V((2, 128, 512), F32), V((3, 2, 1024, 128), F32),
            V((2, 256, 1024), F32), V((3, 2, 128, 1024), F32), V((128, 128), F32),
            V((128, 1024), BF16), V((128, 1024), BF16),
            V((3, 1024, 256), BF16), V((3, 1024, 256), BF16),
            V((256, 2048), BF16), V((256, 2048), BF16),
            V((3, 4, 128, 512), BF16), V((3, 4, 128, 512), BF16),
            V((2, 4, 2, 128, 128), F32), V((2, 32, 32, 128), F32),
            V((16, 1, 128), F32), V((2, 32, 1, 128), F32),
            V((128, 512), F32), V((4, 32, 512), F32), V((128, 512), F32),
            V((3, 512, 128), F32), V((3, 512, 128), F32), V((3, 512, 128), F32),
            V((4, 128, 128), F32), V((8, 64, 128), F32), V((16, 32, 128), F32),
            V((128, 128), F32), V((64, 128), F32), V((32, 128), F32),
            V((1024, 128), F32), V((3, 4, 256, 128), F32), V((128, 128), F32), V((128, 128), F32),
            DMA((8,)), DMA((2,)), DMA((2, 4)), DMA((2,)), DMA((2, 4)), DMA, DMA, DMA((3,)), DMA((3,)),
            DMA((3,)), DMA((3,)), DMA((3,)), DMA((3,)), DMA((3, 4)), DMA,
            DMA((3,)), DMA((3, 3)), DMA((3, 4)), DMA((3, 4)),
        ],
        compiler_params=pltpu.CompilerParams(
            collective_id=0, has_side_effects=True, vmem_limit_bytes=62 * 1024 * 1024
        ),
        name="adjoint_gradient",
    )(
        resid, rec_owner.reshape(8, 128), rec_cell.reshape(8, 128), leaf_inverse[0], couple_up[0],
        sep_inverse[0], couple_down[0], forward_field,
    )
    return out.reshape(128)


def solution(mesh):
    placed = (
        P(("leaf", "front"), None),
        P(("leaf", "front"), None),
        P(("leaf", "front")),
        P("leaf", None, "front", None),
        P("leaf", None, None, None, "front"),
        P("leaf", None, "front", None),
        P("leaf", None, None, "front", None),
        P(("leaf", "front"), None),
    )
    return jax.shard_map(
        local, mesh=mesh, in_specs=placed, out_specs=P(("leaf", "front")), check_vma=False
    )
```

```python
import jax
import jax.numpy as jnp
from jax import lax
from jax.experimental import pallas as pl
from jax.experimental.pallas import tpu as pltpu
from jax.sharding import PartitionSpec as P

F32, BF16, I32 = jnp.float32, jnp.bfloat16, jnp.int32
MESH = pl.DeviceIdType.MESH
DMA = pltpu.SemaphoreType.DMA


def split(value):
    high = value.astype(BF16)
    return high, (value - high.astype(F32)).astype(BF16)


def dot(a, b):
    return jnp.dot(a, b, preferred_element_type=F32)


def dot_rows(a, b):
    return lax.dot_general(a, b, (((1,), (1,)), ((), ())), preferred_element_type=F32)


def rotate(field):
    lane = lax.broadcasted_iota(I32, field.shape, 1)
    turned = pltpu.roll(field, 64, 1)
    return jnp.where(lane < 64, -turned, turned)


def operand(field):
    high, low = split(field)
    turned_high, turned_low = split(rotate(field))
    return jnp.concatenate(
        [jnp.concatenate([high, low], 1), jnp.concatenate([turned_high, turned_low], 1)], 0
    )


def folded(both):
    half = both.shape[0] // 2
    both = both[:, :128] + both[:, 128:]
    return both[:half] + both[half:]


def wait_bytes(ref, sem):
    pltpu.make_async_copy(ref, ref, sem).wait()


def kernel(
    resid, owner_h, cell_h, leaf_inverse, couple_up, sep_inverse, couple_down, field, out,
    owner, cell, resid_v, rows_v, a_f, u_f, s_f, d_f, field_v,
    ap, uh, ul, sp, dp,
    send, recv, meta_send, meta_recv, part, z_recv, source,
    t_send, t_recv, t_sum, r1, r2, r3, s1, s2, s3, pend, sep, acc, fwd,
    load_sem, send_sem, recv_sem, meta_ssem, meta_rsem, zr_ssem, zr_rsem, g_ssem, g_rsem,
    core_ssem, core_rsem, rs_ssem, rs_rsem, p_ssem, p_rsem, z_ssem, b_ssem, h_ssem, f_ssem, b_rsem,
):
    leaf = lax.axis_index("leaf")
    x = lax.axis_index("front")
    c = lax.rem(leaf, 2)
    z = lax.rem(lax.div(leaf, 2), 8)
    y = lax.div(leaf, 16)
    zq, zl = lax.rem(z, 4), lax.rem(z, 2)
    base4, base8 = leaf - lax.rem(leaf, 4), leaf - lax.rem(leaf, 8)
    partner = leaf + 1 - 2 * c

    def remote(src, dst, ssem, rsem, to_leaf, to_front):
        return pltpu.make_async_remote_copy(
            src_ref=src, dst_ref=dst, send_sem=ssem, recv_sem=rsem,
            device_id=(to_leaf, to_front), device_id_type=MESH,
        )

    loads = [
        pltpu.make_async_copy(a, b, load_sem.at[i])
        for i, (a, b) in enumerate(
            [
                (owner_h, owner), (cell_h, cell), (resid, resid_v), (leaf_inverse, a_f), (couple_up, u_f),
                (sep_inverse, s_f), (couple_down, d_f), (field, field_v),
            ]
        )
    ]
    for load in loads:
        load.start()

    barrier = pltpu.get_barrier_semaphore()

    def greet(to_leaf, to_front):
        pl.semaphore_signal(barrier, inc=1, device_id=(to_leaf, to_front), device_id_type=MESH)

    def greet_plane(dy, carry):
        for cd in range(2):
            for dx in (1, 2, 3):
                greet((lax.rem(y + dy, 4) * 8 + z) * 2 + cd, lax.rem(x + dx, 4))
        return carry

    lax.fori_loop(0, 4, greet_plane, 0)

    def greet_column(dy, carry):
        for cd in range(2):
            greet((lax.rem(y + dy, 4) * 8 + z) * 2 + cd, x)
        return carry

    lax.fori_loop(1, 4, greet_column, 0)
    greet(partner, x)

    def greet_column_z(dz, carry):
        greet((y * 8 + lax.rem(z + 2 * dz, 8)) * 2 + c, x)
        return carry

    lax.fori_loop(1, 4, greet_column_z, 0)

    def greet_neighbour(k, carry):
        for dx in range(4):
            greet(lax.rem(k, 4) * 16 + lax.rem(z + 7 + 2 * c, 8) * 2 + lax.div(k, 4), lax.rem(x + dx, 4))
        return carry

    lax.fori_loop(0, 8, greet_neighbour, 0)

    def greet_cube(dz, carry):
        at = base8 + 2 * lax.rem(zq + dz, 4)
        for dx in range(4):
            greet(at + c, lax.rem(x + dx, 4))

            @pl.when(jnp.logical_and(c == 1, jnp.logical_or(zq == 1, jnp.logical_and(zl == 0, dz == 1))))
            def _():
                greet(at, lax.rem(x + dx, 4))

        return carry

    lax.fori_loop(1, 4, greet_cube, 0)

    loads[0].wait()
    loads[1].wait()
    leaf_ids = lax.broadcasted_iota(I32, (64, 128), 0)
    row_id = lax.broadcasted_iota(I32, (128, 128), 0)
    col_id = lax.broadcasted_iota(I32, (128, 128), 1)
    earlier = jnp.where(row_id < col_id, 1.0, 0.0).astype(BF16)
    count = jnp.zeros((64, 1), F32)
    meta = jnp.zeros((32, 128), F32)
    places = []
    for j in range(8):
        own = owner[j : j + 1, :]
        cells = cell[j : j + 1, :]
        member = jnp.where(own == leaf_ids, 1.0, 0.0)
        before = dot(member.astype(BF16), earlier) + count
        rank = jnp.sum(member * before, 0, keepdims=True).astype(I32)
        count = count + jnp.sum(member, 1, keepdims=True)
        places.append(own * 32 + rank)
        line = jnp.right_shift(own, 4) * 4 + jnp.bitwise_and(own, 1) * 2
        line = line + jnp.bitwise_and(jnp.right_shift(own, 1), 1)
        lane = jnp.bitwise_and(jnp.right_shift(own, 2), 3) * 32 + rank
        on_line = jnp.where(line == leaf_ids[:16], 1.0, 0.0)
        low = jnp.bitwise_and(cells, 31)
        parts = jnp.concatenate(
            [on_line * (cells - low).astype(F32), on_line * (low + 1).astype(F32)], 0
        ).astype(BF16)
        meta = meta + dot_rows(parts, jnp.where(lane == row_id, 1.0, 0.0).astype(BF16))
    meta = meta[:16] + meta[16:]
    for i in range(16):
        meta_send[i] = meta[i : i + 1]

    loads[2].wait()
    high, low = split(resid_v[...].T)
    rows_v[:128] = high
    rows_v[128:] = low

    greetings = 31 + 3 + 32 + 12 + (1 - c) * (4 * zl + jnp.where(zq == 1, 0, 4))
    pl.semaphore_wait(barrier, greetings)

    slot = lax.broadcasted_iota(I32, (256, 128), 0)
    slot = (
        jnp.bitwise_and(jnp.right_shift(slot, 7), 1) * 32
        + jnp.bitwise_and(jnp.right_shift(slot, 5), 3) * 128
        + jnp.bitwise_and(slot, 31)
    )
    me_plane = y * 8 + x * 2 + c
    for h in (1, 0):
        parity = lax.rem(z + h, 2)
        for dy in (2, 1, 3, 0):
            yd = lax.rem(y + dy, 4)
            slots = slot + (yd * 512 + parity * 64)
            pick = jnp.concatenate(
                [jnp.where(place == slots, 1.0, 0.0).astype(BF16) for place in places], 1
            )
            rows = dot_rows(rows_v[...], pick)
            rows = rows[:128] + rows[128:]
            for cd in range(2):
                send[h, dy, cd] = rows[:, cd * 128 : cd * 128 + 128]

            def push(k, carry):
                xt = lax.rem(x + 2 + lax.div(k, 2), 4)
                cd = lax.rem(c + lax.rem(k, 2), 2)
                zt = lax.rem(z + 1 + 6 * cd, 8) if h else z
                to = (yd * 8 + zt) * 2 + cd
                src = send.at[h, dy, cd, pl.ds(pl.multiple_of(xt * 32, 32), 32)]
                dst = recv.at[h, me_plane]
                meta_src = meta_send.at[yd * 4 + cd * 2 + parity]
                meta_dst = meta_recv.at[h, me_plane]

                def far():
                    remote(meta_src, meta_dst, meta_ssem.at[h], meta_rsem.at[h, y], to, xt).start()
                    remote(src, dst, send_sem.at[h], recv_sem.at[h, y], to, xt).start()

                def near():
                    pltpu.make_async_copy(meta_src, meta_dst, meta_rsem.at[h, y]).start()
                    pltpu.make_async_copy(src, dst, recv_sem.at[h, y]).start()

                if dy or h:
                    far()
                else:
                    self_copy = jnp.logical_and(to == leaf, xt == x)
                    pl.when(jnp.logical_not(self_copy))(far)
                    pl.when(self_copy)(near)
                return carry

            lax.fori_loop(0, 8, push, 0)

    for load in loads[3:]:
        load.wait()
    for m in range(2):
        high, low = split(a_f[m])
        ap[:128, m * 512 : m * 512 + 512] = high
        ap[128:, m * 512 : m * 512 + 512] = low

    def split_up(i, carry):
        level, at = lax.div(i, 8), pl.ds(pl.multiple_of(lax.rem(i, 8) * 128, 128), 128)
        for m in range(2):
            high, low = split(u_f[level, m, at])
            uh[level, at, m * 128 : m * 128 + 128] = high
            ul[level, at, m * 128 : m * 128 + 128] = low
        return carry

    lax.fori_loop(0, 24, split_up, 0)

    def split_sep(i, carry):
        start = pl.multiple_of(i * 32, 32)
        for m in range(2):
            for q in range(4):
                high, low = split(s_f[m, pl.ds(start, 32), q * 256 : q * 256 + 256])
                sp[q, pl.ds(start, 32), m * 256 : m * 256 + 256] = high
                sp[q, pl.ds(start + 256, 32), m * 256 : m * 256 + 256] = low
        return carry

    lax.fori_loop(0, 8, split_sep, 0)

    def split_down(i, carry):
        level, start = lax.div(i, 4), pl.multiple_of(lax.rem(i, 4) * 32, 32)
        for m in range(2):
            for f in range(4):
                high, low = split(d_f[level, m, pl.ds(start, 32), f * 256 : f * 256 + 256])
                dp[level, f, pl.ds(start, 32), m * 256 : m * 256 + 256] = high
                dp[level, f, pl.ds(start + 128, 32), m * 256 : m * 256 + 256] = low
        return carry

    lax.fori_loop(0, 12, split_down, 0)

    cell_ids = lax.broadcasted_iota(I32, (512, 128), 0) + 1
    diagonal = jnp.where(jnp.right_shift(row_id, 5) == jnp.right_shift(col_id, 5), 1.0, 0.0)
    diagonal = diagonal.astype(BF16)
    for h in (1, 0):
        for dy in (2, 1, 3, 0):
            ys = lax.rem(y + 4 - dy, 4)
            wait_bytes(meta_recv.at[h, pl.ds(ys * 8, 8)], meta_rsem.at[h, ys])
            wait_bytes(recv.at[h, pl.ds(ys * 8, 8)], recv_sem.at[h, ys])
            hits, values = [], []
            for i in range(8):
                line = meta_recv[h, ys * 8 + i].astype(I32)
                hits.append(jnp.where(line == cell_ids, 1.0, 0.0).astype(BF16))
                values.append(
                    jnp.concatenate(
                        [
                            jnp.concatenate([piece] * 4, 0) * diagonal
                            for piece in split(recv[h, ys * 8 + i])
                        ],
                        0,
                    )
                )
            both = dot_rows(jnp.concatenate(values, 1), jnp.concatenate(hits, 1))
            both = both[:128] + both[128:]
            if h and dy == 2:
                part[...] = both
            else:
                part[...] += both

    zh = lax.div(z, 2)
    for half in range(2):
        for i in (2, 1, 3, 0):
            zd = lax.rem(z + 2 * i, 8)
            at = pl.multiple_of(lax.div(zd, 2) * 32 + half * 16, 16)
            src, dst = part.at[pl.ds(at, 16)], z_recv.at[half, zh]
            if i:
                to = (y * 8 + zd) * 2 + c
                remote(src, dst, zr_ssem.at[half], zr_rsem.at[half], to, x).start()
            else:
                pltpu.make_async_copy(src, dst, zr_rsem.at[half]).start()

    gather = []
    for half in range(2):
        mine = pl.ds(pl.multiple_of(x * 32 + half * 16, 16), 16)
        wait_bytes(z_recv.at[half], zr_rsem.at[half])
        total = z_recv[half, 0]
        for i in range(1, 4):
            total = total + z_recv[half, i]
        source[mine] = total
        for dx in (2, 1, 3):
            copy = remote(
                source.at[mine], source.at[mine], g_ssem.at[half, dx - 1], g_rsem.at[half, dx - 1],
                leaf, lax.rem(x + dx, 4),
            )
            copy.start()
            gather.append(copy)
    for copy in gather:
        copy.wait_recv()

    high, low = split(source[...])
    right = jnp.concatenate(
        [jnp.concatenate([p, jnp.concatenate([-p[64:], p[:64]], 0)], 1) for p in (high, low)], 0
    )
    forward = folded(dot_rows(ap[...], right))
    fwd[...] = forward
    right = operand(-forward)

    swaps = [
        remote(t_send.at[k], t_recv.at[k], core_ssem.at[k], core_rsem.at[k], partner, x)
        for k in range(3)
    ]
    theirs = pl.ds(pl.multiple_of((1 - c) * 512, 512), 512)
    ours = pl.ds(pl.multiple_of(c * 512, 512), 512)
    stages = ((r1, s1, 1, 128, 0), (r2, s2, 2, 64, zl), (r3, s3, 4, 32, zq))

    def term(k, at):
        both = dot(uh[k, at], right)
        return both[:, :128] + both[:, 128:] + dot(ul[k, at], right[:, :128])

    def give(k):
        t_send[k] = term(k, theirs)
        swaps[k].start()

    def scatter(k):
        box, _, span, rows, zk = stages[k]
        swaps[k].wait_recv()
        t_sum[k] += t_recv[k]
        me = zk * 4 + x
        for dz in range(span):
            for dx in (2, 1, 3, 0):
                if dz or dx:
                    zt = lax.rem(zk + dz, span)
                    xt = lax.rem(x + dx, 4)
                    at = pl.ds(pl.multiple_of((zt * 4 + xt) * rows, rows), rows)
                    remote(
                        t_sum.at[k, at], box.at[me], rs_ssem.at[k], rs_rsem.at[k],
                        leaf + 2 * (zt - zk), xt,
                    ).start()
        box[me] = t_sum[k, pl.ds(pl.multiple_of(me * rows, rows), rows)]

    give(0)
    t_sum[0] = term(0, ours)
    give(2)
    scatter(0)
    t_sum[2] = term(2, ours)
    give(1)
    scatter(2)
    t_sum[1] = term(1, ours)
    scatter(1)

    targets = (leaf - c, base4 + 1, base8 + 3)
    for k in (0, 2, 1):
        box, total, span, rows, zk = stages[k]
        wait_bytes(box.at[pl.ds(0, 4 * span - 1)], rs_rsem.at[k])
        value = box[0]
        for i in range(1, 4 * span):
            value = value + box[i]
        total[...] = value
        at = pl.ds(pl.multiple_of(c * 512 + (zk * 4 + x) * rows, rows), rows)
        quarter = c * 2 + lax.div(zk * 4 + x, 2 * span)
        for f in range(4):
            local_one = jnp.logical_and(targets[k] == leaf, x == f)

            def far(k=k, f=f, total=total, at=at, quarter=quarter):
                remote(total, pend.at[at], p_ssem.at[k, f], p_rsem.at[quarter], targets[k], f).start()

            def near(k=k, f=f, total=total, at=at, quarter=quarter):
                pltpu.make_async_copy(total, pend.at[at], p_rsem.at[quarter]).start()

            pl.when(jnp.logical_not(local_one))(far)
            pl.when(local_one)(near)

    owns = lax.rem(leaf, 8) != 7
    level_own = jnp.where(c == 0, 0, jnp.where(zl == 0, 1, 2))

    @pl.when(owns)
    def _():
        both = None
        for q in range(4):
            at = pl.ds(q * 256, 256)
            wait_bytes(pend.at[at], p_rsem.at[q])
            more = dot(sp[q], operand(pend[at]))
            both = more if both is None else both + more
        sep[level_own, x] = folded(both)

    def along_x(k):
        for dx in (1, 3):
            xt = lax.rem(x + dx, 4)
            remote(sep.at[k, x], sep.at[k, x], b_ssem.at[k, dx - 1], b_rsem.at[k, x], leaf, xt).start()

    def relay(k, f, dx):
        if dx != 2:
            part_ref = sep.at[k, f, pl.ds(0 if dx == 1 else 128, 128)]
            remote(
                part_ref, part_ref, h_ssem.at[k, dx // 2], b_rsem.at[k, f],
                leaf, lax.rem(x + 4 - dx, 4),
            ).start()

    def across(k, f):
        remote(sep.at[k, f], sep.at[k, f], f_ssem.at[k, f], b_rsem.at[k, f], partner, x).start()

    def arrived(k, f):
        wait_bytes(sep.at[k, f], b_rsem.at[k, f])

    def along_z(k, i, to):
        return remote(sep.at[k, x], sep.at[k, x], z_ssem.at[i], b_rsem.at[k, x], to, x)

    z_sends2 = (along_z(1, 0, leaf + 2),)
    z_sends3 = (along_z(2, 0, base8 + 7), along_z(2, 1, base8 + 5), along_z(2, 2, base8 + 1))
    is2 = jnp.logical_and(c == 1, zl == 0)
    is3 = jnp.logical_and(c == 1, zq == 1)

    @pl.when(is2)
    def _():
        for copy in z_sends2:
            copy.start()

    @pl.when(is3)
    def _():
        for copy in z_sends3:
            copy.start()

    @pl.when(c == 0)
    def _():
        along_x(0)
        across(0, x)

    @pl.when(is2)
    def _():
        along_x(1)
        across(1, x)
        arrived(2, x)
        along_x(2)
        across(2, x)

    @pl.when(is3)
    def _():
        along_x(2)
        across(2, x)
        arrived(1, x)
        along_x(1)
        across(1, x)

    @pl.when(jnp.logical_and(c == 1, zq == 3))
    def _():
        for k in (1, 2):
            arrived(k, x)
            along_x(k)
            across(k, x)

    acc[...] = jnp.zeros_like(acc)

    def consume(f):
        for k in range(3):
            acc[...] += folded(dot(dp[k, f], operand(sep[k, f])))

    def take(k, dx):
        f = lax.rem(x + dx, 4)
        arrived(k, f)
        relay(k, f, dx)
        across(k, f)

    def take_all(steps):
        @pl.when(c == 0)
        def _():
            for dx in steps:
                take(0, dx)

        @pl.when(is3)
        def _():
            for k in (2, 1):
                for dx in steps:
                    take(k, dx)

        @pl.when(jnp.logical_and(c == 1, zq != 1))
        def _():
            for k in (1, 2):
                for dx in steps:
                    take(k, dx)

    def use(dx):
        f = lax.rem(x + dx, 4)

        @pl.when(c == 0)
        def _():
            for k in (1, 2):
                arrived(k, f)

        @pl.when(c == 1)
        def _():
            arrived(0, f)

        consume(f)

    take_all((1, 3))
    use(0)
    use(1)
    use(3)
    take_all((2,))
    use(2)

    weight = jnp.where(col_id < 64, 0.125, -0.125)
    value = field_v[...] * (fwd[...] - acc[...]) * weight
    out[...] = jnp.sum(value.T, 0, keepdims=True)

    for h in range(2):
        wait_bytes(recv.at[h, pl.ds(0, 31 + h)], send_sem.at[h])
        wait_bytes(meta_recv.at[h, pl.ds(0, 31 + h)], meta_ssem.at[h])
    for half in range(2):
        wait_bytes(z_recv.at[half, pl.ds(0, 3)], zr_ssem.at[half])
    for copy in gather + swaps:
        copy.wait_send()
    for k in range(3):
        box, total, span, rows, zk = stages[k]
        wait_bytes(box.at[pl.ds(0, 4 * span - 1)], rs_ssem.at[k])
        for f in range(4):
            local_one = jnp.logical_and(targets[k] == leaf, x == f)

            @pl.when(jnp.logical_not(local_one))
            def _(k=k, f=f, total=total):
                wait_bytes(total, p_ssem.at[k, f])

    @pl.when(is2)
    def _():
        for copy in z_sends2:
            copy.wait_send()

    @pl.when(is3)
    def _():
        for copy in z_sends3:
            copy.wait_send()

    def drain(k):
        for dx in (1, 3):
            wait_bytes(sep.at[k, x], b_ssem.at[k, dx - 1])
            wait_bytes(sep.at[k, x, pl.ds(0, 128)], h_ssem.at[k, dx // 2])
        for f in range(4):
            wait_bytes(sep.at[k, f], f_ssem.at[k, f])

    @pl.when(c == 0)
    def _():
        drain(0)

    @pl.when(c == 1)
    def _():
        drain(1)
        drain(2)


def local(
    resid, rec_owner, rec_cell, leaf_inverse, couple_up, sep_inverse, couple_down, forward_field
):
    vmem = pl.BlockSpec(memory_space=pltpu.VMEM)
    hbm = pl.BlockSpec(memory_space=pl.ANY)
    V = pltpu.VMEM
    out = pl.pallas_call(
        kernel,
        out_shape=jax.ShapeDtypeStruct((1, 128), F32),
        in_specs=[hbm] * 8,
        out_specs=vmem,
        scratch_shapes=[
            V((8, 128), I32), V((8, 128), I32), V((1024, 128), F32), V((256, 1024), BF16),
            V((2, 128, 512), F32), V((3, 2, 1024, 128), F32),
            V((2, 256, 1024), F32), V((3, 2, 128, 1024), F32), V((128, 128), F32),
            V((256, 1024), BF16),
            V((3, 1024, 256), BF16), V((3, 1024, 256), BF16),
            V((4, 512, 512), BF16), V((3, 4, 256, 512), BF16),
            V((2, 4, 2, 128, 128), F32), V((2, 32, 32, 128), F32),
            V((16, 1, 128), F32), V((2, 32, 1, 128), F32),
            V((128, 512), F32), V((2, 4, 16, 512), F32), V((128, 512), F32),
            V((3, 512, 128), F32), V((3, 512, 128), F32), V((3, 512, 128), F32),
            V((4, 128, 128), F32), V((8, 64, 128), F32), V((16, 32, 128), F32),
            V((128, 128), F32), V((64, 128), F32), V((32, 128), F32),
            V((1024, 128), F32), V((3, 4, 256, 128), F32), V((128, 128), F32), V((128, 128), F32),
            DMA((8,)), DMA((2,)), DMA((2, 4)), DMA((2,)), DMA((2, 4)), DMA((2,)), DMA((2,)), DMA((2, 3)), DMA((2, 3)),
            DMA((3,)), DMA((3,)), DMA((3,)), DMA((3,)), DMA((3, 4)), DMA((4,)),
            DMA((3,)), DMA((3, 3)), DMA((3, 2)), DMA((3, 4)), DMA((3, 4)),
        ],
        compiler_params=pltpu.CompilerParams(
            collective_id=0, has_side_effects=True, vmem_limit_bytes=62 * 1024 * 1024
        ),
        name="adjoint_gradient",
    )(
        resid, rec_owner.reshape(8, 128), rec_cell.reshape(8, 128), leaf_inverse[0], couple_up[0],
        sep_inverse[0], couple_down[0], forward_field,
    )
    return out.reshape(128)


def solution(mesh):
    placed = (
        P(("leaf", "front"), None),
        P(("leaf", "front"), None),
        P(("leaf", "front")),
        P("leaf", None, "front", None),
        P("leaf", None, None, None, "front"),
        P("leaf", None, "front", None),
        P("leaf", None, None, "front", None),
        P(("leaf", "front"), None),
    )
    return jax.shard_map(
        local, mesh=mesh, in_specs=placed, out_specs=P(("leaf", "front")), check_vma=False
    )
```

```python
import jax
import jax.numpy as jnp
from jax import lax
from jax.experimental import pallas as pl
from jax.experimental.pallas import tpu as pltpu
from jax.sharding import PartitionSpec as P

F32, BF16, I32 = jnp.float32, jnp.bfloat16, jnp.int32
MESH = pl.DeviceIdType.MESH
DMA = pltpu.SemaphoreType.DMA


def split(value):
    high = value.astype(BF16)
    return high, (value - high.astype(F32)).astype(BF16)


def dot(a, b):
    return jnp.dot(a, b, preferred_element_type=F32)


def dot_rows(a, b):
    return lax.dot_general(a, b, (((1,), (1,)), ((), ())), preferred_element_type=F32)


def rotate(field):
    lane = lax.broadcasted_iota(I32, field.shape, 1)
    turned = pltpu.roll(field, 64, 1)
    return jnp.where(lane < 64, -turned, turned)


def operand(field):
    high, low = split(field)
    turned_high, turned_low = split(rotate(field))
    return jnp.concatenate(
        [jnp.concatenate([high, low], 1), jnp.concatenate([turned_high, turned_low], 1)], 0
    )


def folded(both):
    half = both.shape[0] // 2
    both = both[:, :128] + both[:, 128:]
    return both[:half] + both[half:]


def wait_bytes(ref, sem):
    pltpu.make_async_copy(ref, ref, sem).wait()


def kernel(
    resid, owner_h, cell_h, leaf_inverse, couple_up, sep_inverse, couple_down, field, out,
    owner, cell, resid_v, rows_v, a_f, u_f, s_f, d_f, field_v,
    ap, uh, ul, sp, dp,
    send, recv, meta_send, meta_recv, part, z_recv, source,
    t_send, t_recv, t_sum, r1, r2, r3, s1, s2, s3, pend, sep, acc, fwd,
    load_sem, send_sem, recv_sem, meta_ssem, meta_rsem, zr_ssem, zr_rsem, g_ssem, g_rsem,
    core_ssem, core_rsem, rs_ssem, rs_rsem, p_ssem, p_rsem, z_ssem, b_ssem, h_ssem, f_ssem, b_rsem,
):
    leaf = lax.axis_index("leaf")
    x = lax.axis_index("front")
    c = lax.rem(leaf, 2)
    z = lax.rem(lax.div(leaf, 2), 8)
    y = lax.div(leaf, 16)
    zq, zl = lax.rem(z, 4), lax.rem(z, 2)
    base4, base8 = leaf - lax.rem(leaf, 4), leaf - lax.rem(leaf, 8)
    partner = leaf + 1 - 2 * c

    def remote(src, dst, ssem, rsem, to_leaf, to_front):
        return pltpu.make_async_remote_copy(
            src_ref=src, dst_ref=dst, send_sem=ssem, recv_sem=rsem,
            device_id=(to_leaf, to_front), device_id_type=MESH,
        )

    loads = [
        pltpu.make_async_copy(a, b, load_sem.at[i])
        for i, (a, b) in enumerate(
            [
                (owner_h, owner), (cell_h, cell), (resid, resid_v), (leaf_inverse, a_f), (couple_up, u_f),
                (sep_inverse, s_f), (couple_down, d_f), (field, field_v),
            ]
        )
    ]
    for load in loads:
        load.start()

    barrier = pltpu.get_barrier_semaphore()

    def greet(to_leaf, to_front):
        pl.semaphore_signal(barrier, inc=1, device_id=(to_leaf, to_front), device_id_type=MESH)

    def greet_plane(dy, carry):
        for cd in range(2):
            for dx in (1, 2, 3):
                greet((lax.rem(y + dy, 4) * 8 + z) * 2 + cd, lax.rem(x + dx, 4))
        return carry

    lax.fori_loop(0, 4, greet_plane, 0)

    def greet_column(dy, carry):
        for cd in range(2):
            greet((lax.rem(y + dy, 4) * 8 + z) * 2 + cd, x)
        return carry

    lax.fori_loop(1, 4, greet_column, 0)
    greet(partner, x)

    def greet_column_z(dz, carry):
        greet((y * 8 + lax.rem(z + 2 * dz, 8)) * 2 + c, x)
        return carry

    lax.fori_loop(1, 4, greet_column_z, 0)

    def greet_neighbour(k, carry):
        for dx in range(4):
            greet(lax.rem(k, 4) * 16 + lax.rem(z + 7 + 2 * c, 8) * 2 + lax.div(k, 4), lax.rem(x + dx, 4))
        return carry

    lax.fori_loop(0, 8, greet_neighbour, 0)

    def greet_cube(dz, carry):
        at = base8 + 2 * lax.rem(zq + dz, 4)
        for dx in range(4):
            greet(at + c, lax.rem(x + dx, 4))

            @pl.when(jnp.logical_and(c == 1, jnp.logical_or(zq == 1, jnp.logical_and(zl == 0, dz == 1))))
            def _():
                greet(at, lax.rem(x + dx, 4))

        return carry

    lax.fori_loop(1, 4, greet_cube, 0)

    loads[0].wait()
    loads[1].wait()
    leaf_ids = lax.broadcasted_iota(I32, (64, 128), 0)
    row_id = lax.broadcasted_iota(I32, (128, 128), 0)
    col_id = lax.broadcasted_iota(I32, (128, 128), 1)
    earlier = jnp.where(row_id < col_id, 1.0, 0.0).astype(BF16)
    count = jnp.zeros((64, 1), F32)
    meta = jnp.zeros((32, 128), F32)
    places = []
    for j in range(8):
        own = owner[j : j + 1, :]
        cells = cell[j : j + 1, :]
        member = jnp.where(own == leaf_ids, 1.0, 0.0)
        before = dot(member.astype(BF16), earlier) + count
        rank = jnp.sum(member * before, 0, keepdims=True).astype(I32)
        count = count + jnp.sum(member, 1, keepdims=True)
        places.append(own * 32 + rank)
        line = jnp.right_shift(own, 4) * 4 + jnp.bitwise_and(own, 1) * 2
        line = line + jnp.bitwise_and(jnp.right_shift(own, 1), 1)
        lane = jnp.bitwise_and(jnp.right_shift(own, 2), 3) * 32 + rank
        on_line = jnp.where(line == leaf_ids[:16], 1.0, 0.0)
        low = jnp.bitwise_and(cells, 31)
        parts = jnp.concatenate(
            [on_line * (cells - low).astype(F32), on_line * (low + 1).astype(F32)], 0
        ).astype(BF16)
        meta = meta + dot_rows(parts, jnp.where(lane == row_id, 1.0, 0.0).astype(BF16))
    meta = meta[:16] + meta[16:]
    for i in range(16):
        meta_send[i] = meta[i : i + 1]

    loads[2].wait()
    high, low = split(resid_v[...].T)
    rows_v[:128] = high
    rows_v[128:] = low

    greetings = 31 + 3 + 32 + 12 + (1 - c) * (4 * zl + jnp.where(zq == 1, 0, 4))
    pl.semaphore_wait(barrier, greetings)

    slot = lax.broadcasted_iota(I32, (256, 128), 0)
    slot = (
        jnp.bitwise_and(jnp.right_shift(slot, 7), 1) * 32
        + jnp.bitwise_and(jnp.right_shift(slot, 5), 3) * 128
        + jnp.bitwise_and(slot, 31)
    )
    me_plane = y * 8 + x * 2 + c
    for h in (1, 0):
        parity = lax.rem(z + h, 2)
        for dy in (2, 1, 3, 0):
            yd = lax.rem(y + dy, 4)
            slots = slot + (yd * 512 + parity * 64)
            pick = jnp.concatenate(
                [jnp.where(place == slots, 1.0, 0.0).astype(BF16) for place in places], 1
            )
            rows = dot_rows(rows_v[...], pick)
            rows = rows[:128] + rows[128:]
            for cd in range(2):
                send[h, dy, cd] = rows[:, cd * 128 : cd * 128 + 128]

            def push(k, carry):
                xt = lax.rem(x + 2 + lax.div(k, 2), 4)
                cd = lax.rem(c + lax.rem(k, 2), 2)
                zt = lax.rem(z + 1 + 6 * cd, 8) if h else z
                to = (yd * 8 + zt) * 2 + cd
                src = send.at[h, dy, cd, pl.ds(pl.multiple_of(xt * 32, 32), 32)]
                dst = recv.at[h, me_plane]
                meta_src = meta_send.at[yd * 4 + cd * 2 + parity]
                meta_dst = meta_recv.at[h, me_plane]

                def far():
                    remote(meta_src, meta_dst, meta_ssem.at[h], meta_rsem.at[h, y], to, xt).start()
                    remote(src, dst, send_sem.at[h], recv_sem.at[h, y], to, xt).start()

                def near():
                    pltpu.make_async_copy(meta_src, meta_dst, meta_rsem.at[h, y]).start()
                    pltpu.make_async_copy(src, dst, recv_sem.at[h, y]).start()

                if dy or h:
                    far()
                else:
                    self_copy = jnp.logical_and(to == leaf, xt == x)
                    pl.when(jnp.logical_not(self_copy))(far)
                    pl.when(self_copy)(near)
                return carry

            lax.fori_loop(0, 8, push, 0)

    for load in loads[3:]:
        load.wait()
    for m in range(2):
        high, low = split(a_f[m])
        ap[:128, m * 512 : m * 512 + 512] = high
        ap[128:, m * 512 : m * 512 + 512] = low

    def split_up(i, carry):
        level, at = lax.div(i, 8), pl.ds(pl.multiple_of(lax.rem(i, 8) * 128, 128), 128)
        for m in range(2):
            high, low = split(u_f[level, m, at])
            uh[level, at, m * 128 : m * 128 + 128] = high
            ul[level, at, m * 128 : m * 128 + 128] = low
        return carry

    lax.fori_loop(0, 24, split_up, 0)

    def split_sep(i, carry):
        start = pl.multiple_of(i * 32, 32)
        for m in range(2):
            for q in range(4):
                high, low = split(s_f[m, pl.ds(start, 32), q * 256 : q * 256 + 256])
                sp[q, pl.ds(start, 32), m * 256 : m * 256 + 256] = high
                sp[q, pl.ds(start + 256, 32), m * 256 : m * 256 + 256] = low
        return carry

    lax.fori_loop(0, 8, split_sep, 0)

    def split_down(i, carry):
        level, start = lax.div(i, 4), pl.multiple_of(lax.rem(i, 4) * 32, 32)
        for m in range(2):
            for f in range(4):
                high, low = split(d_f[level, m, pl.ds(start, 32), f * 256 : f * 256 + 256])
                dp[level, f, pl.ds(start, 32), m * 256 : m * 256 + 256] = high
                dp[level, f, pl.ds(start + 128, 32), m * 256 : m * 256 + 256] = low
        return carry

    lax.fori_loop(0, 12, split_down, 0)

    cell_ids = lax.broadcasted_iota(I32, (512, 128), 0) + 1
    diagonal = jnp.where(jnp.right_shift(row_id, 5) == jnp.right_shift(col_id, 5), 1.0, 0.0)
    diagonal = diagonal.astype(BF16)
    for h in (1, 0):
        for dy in (2, 1, 3, 0):
            ys = lax.rem(y + 4 - dy, 4)
            wait_bytes(meta_recv.at[h, pl.ds(ys * 8, 8)], meta_rsem.at[h, ys])
            wait_bytes(recv.at[h, pl.ds(ys * 8, 8)], recv_sem.at[h, ys])
            hits, values = [], []
            for i in range(8):
                line = meta_recv[h, ys * 8 + i].astype(I32)
                hits.append(jnp.where(line == cell_ids, 1.0, 0.0).astype(BF16))
                values.append(
                    jnp.concatenate(
                        [
                            jnp.concatenate([piece] * 4, 0) * diagonal
                            for piece in split(recv[h, ys * 8 + i])
                        ],
                        0,
                    )
                )
            both = dot_rows(jnp.concatenate(values, 1), jnp.concatenate(hits, 1))
            both = both[:128] + both[128:]
            if h and dy == 2:
                part[...] = both
            else:
                part[...] += both

    zh = lax.div(z, 2)
    for half in range(2):
        for i in (2, 1, 3, 0):
            zd = lax.rem(z + 2 * i, 8)
            at = pl.multiple_of(lax.div(zd, 2) * 32 + half * 16, 16)
            src, dst = part.at[pl.ds(at, 16)], z_recv.at[half, zh]
            if i:
                to = (y * 8 + zd) * 2 + c
                remote(src, dst, zr_ssem.at[half], zr_rsem.at[half], to, x).start()
            else:
                pltpu.make_async_copy(src, dst, zr_rsem.at[half]).start()

    gather = []
    for half in range(2):
        mine = pl.ds(pl.multiple_of(x * 32 + half * 16, 16), 16)
        wait_bytes(z_recv.at[half], zr_rsem.at[half])
        total = z_recv[half, 0]
        for i in range(1, 4):
            total = total + z_recv[half, i]
        source[mine] = total
        for dx in (2, 1, 3):
            copy = remote(
                source.at[mine], source.at[mine], g_ssem.at[half, dx - 1], g_rsem.at[half, dx - 1],
                leaf, lax.rem(x + dx, 4),
            )
            copy.start()
            gather.append(copy)
    for copy in gather:
        copy.wait_recv()

    high, low = split(source[...])
    right = jnp.concatenate(
        [jnp.concatenate([p, jnp.concatenate([-p[64:], p[:64]], 0)], 1) for p in (high, low)], 0
    )
    forward = folded(dot_rows(ap[...], right))
    fwd[...] = forward
    right = operand(-forward)

    swaps = [
        remote(t_send.at[k], t_recv.at[k], core_ssem.at[k], core_rsem.at[k], partner, x)
        for k in range(3)
    ]
    theirs = pl.ds(pl.multiple_of((1 - c) * 512, 512), 512)
    ours = pl.ds(pl.multiple_of(c * 512, 512), 512)
    stages = ((r1, s1, 1, 128, 0), (r2, s2, 2, 64, zl), (r3, s3, 4, 32, zq))

    def term(k, at):
        both = dot(uh[k, at], right)
        return both[:, :128] + both[:, 128:] + dot(ul[k, at], right[:, :128])

    def give(k):
        t_send[k] = term(k, theirs)
        swaps[k].start()

    def scatter(k):
        box, _, span, rows, zk = stages[k]
        swaps[k].wait_recv()
        t_sum[k] += t_recv[k]
        me = zk * 4 + x
        for dz in range(span):
            for dx in (2, 1, 3, 0):
                if dz or dx:
                    zt = lax.rem(zk + dz, span)
                    xt = lax.rem(x + dx, 4)
                    at = pl.ds(pl.multiple_of((zt * 4 + xt) * rows, rows), rows)
                    remote(
                        t_sum.at[k, at], box.at[me], rs_ssem.at[k], rs_rsem.at[k],
                        leaf + 2 * (zt - zk), xt,
                    ).start()
        box[me] = t_sum[k, pl.ds(pl.multiple_of(me * rows, rows), rows)]

    give(2)
    t_sum[2] = term(2, ours)
    give(0)
    scatter(2)
    t_sum[0] = term(0, ours)
    give(1)
    scatter(0)
    t_sum[1] = term(1, ours)
    scatter(1)

    targets = (leaf - c, base4 + 1, base8 + 3)
    for k in (2, 0, 1):
        box, total, span, rows, zk = stages[k]
        wait_bytes(box.at[pl.ds(0, 4 * span - 1)], rs_rsem.at[k])
        value = box[0]
        for i in range(1, 4 * span):
            value = value + box[i]
        total[...] = value
        at = pl.ds(pl.multiple_of(c * 512 + (zk * 4 + x) * rows, rows), rows)
        quarter = c * 2 + lax.div(zk * 4 + x, 2 * span)
        for f in range(4):
            local_one = jnp.logical_and(targets[k] == leaf, x == f)

            def far(k=k, f=f, total=total, at=at, quarter=quarter):
                remote(total, pend.at[at], p_ssem.at[k, f], p_rsem.at[quarter], targets[k], f).start()

            def near(k=k, f=f, total=total, at=at, quarter=quarter):
                pltpu.make_async_copy(total, pend.at[at], p_rsem.at[quarter]).start()

            pl.when(jnp.logical_not(local_one))(far)
            pl.when(local_one)(near)

    owns = lax.rem(leaf, 8) != 7
    level_own = jnp.where(c == 0, 0, jnp.where(zl == 0, 1, 2))

    @pl.when(owns)
    def _():
        both = None
        for q in range(4):
            at = pl.ds(q * 256, 256)
            wait_bytes(pend.at[at], p_rsem.at[q])
            more = dot(sp[q], operand(pend[at]))
            both = more if both is None else both + more
        sep[level_own, x] = folded(both)

    def along_x(k):
        for dx in (1, 3):
            xt = lax.rem(x + dx, 4)
            remote(sep.at[k, x], sep.at[k, x], b_ssem.at[k, dx - 1], b_rsem.at[k, x], leaf, xt).start()

    def relay(k, f, dx):
        if dx != 2:
            part_ref = sep.at[k, f, pl.ds(0 if dx == 1 else 128, 128)]
            remote(
                part_ref, part_ref, h_ssem.at[k, dx // 2], b_rsem.at[k, f],
                leaf, lax.rem(x + 4 - dx, 4),
            ).start()

    def across(k, f):
        remote(sep.at[k, f], sep.at[k, f], f_ssem.at[k, f], b_rsem.at[k, f], partner, x).start()

    def arrived(k, f):
        wait_bytes(sep.at[k, f], b_rsem.at[k, f])

    def along_z(k, i, to):
        return remote(sep.at[k, x], sep.at[k, x], z_ssem.at[i], b_rsem.at[k, x], to, x)

    z_sends2 = (along_z(1, 0, leaf + 2),)
    z_sends3 = (along_z(2, 0, base8 + 7), along_z(2, 1, base8 + 5), along_z(2, 2, base8 + 1))
    is2 = jnp.logical_and(c == 1, zl == 0)
    is3 = jnp.logical_and(c == 1, zq == 1)

    @pl.when(is2)
    def _():
        for copy in z_sends2:
            copy.start()

    @pl.when(is3)
    def _():
        for copy in z_sends3:
            copy.start()

    @pl.when(c == 0)
    def _():
        along_x(0)
        across(0, x)

    @pl.when(is2)
    def _():
        along_x(1)
        across(1, x)
        arrived(2, x)
        along_x(2)
        across(2, x)

    @pl.when(is3)
    def _():
        along_x(2)
        across(2, x)
        arrived(1, x)
        along_x(1)
        across(1, x)

    @pl.when(jnp.logical_and(c == 1, zq == 3))
    def _():
        for k in (1, 2):
            arrived(k, x)
            along_x(k)
            across(k, x)

    acc[...] = jnp.zeros_like(acc)

    def consume(f):
        for k in range(3):
            acc[...] += folded(dot(dp[k, f], operand(sep[k, f])))

    def take(k, dx):
        f = lax.rem(x + dx, 4)
        arrived(k, f)
        relay(k, f, dx)
        across(k, f)

    def take_all(steps):
        @pl.when(c == 0)
        def _():
            for dx in steps:
                take(0, dx)

        @pl.when(is3)
        def _():
            for k in (2, 1):
                for dx in steps:
                    take(k, dx)

        @pl.when(jnp.logical_and(c == 1, zq != 1))
        def _():
            for k in (1, 2):
                for dx in steps:
                    take(k, dx)

    def use(dx):
        f = lax.rem(x + dx, 4)

        @pl.when(c == 0)
        def _():
            for k in (1, 2):
                arrived(k, f)

        @pl.when(c == 1)
        def _():
            arrived(0, f)

        consume(f)

    take_all((1, 3))
    use(0)
    use(1)
    use(3)
    take_all((2,))
    use(2)

    weight = jnp.where(col_id < 64, 0.125, -0.125)
    value = field_v[...] * (fwd[...] - acc[...]) * weight
    out[...] = jnp.sum(value.T, 0, keepdims=True)

    for h in range(2):
        wait_bytes(recv.at[h, pl.ds(0, 31 + h)], send_sem.at[h])
        wait_bytes(meta_recv.at[h, pl.ds(0, 31 + h)], meta_ssem.at[h])
    for half in range(2):
        wait_bytes(z_recv.at[half, pl.ds(0, 3)], zr_ssem.at[half])
    for copy in gather + swaps:
        copy.wait_send()
    for k in range(3):
        box, total, span, rows, zk = stages[k]
        wait_bytes(box.at[pl.ds(0, 4 * span - 1)], rs_ssem.at[k])
        for f in range(4):
            local_one = jnp.logical_and(targets[k] == leaf, x == f)

            @pl.when(jnp.logical_not(local_one))
            def _(k=k, f=f, total=total):
                wait_bytes(total, p_ssem.at[k, f])

    @pl.when(is2)
    def _():
        for copy in z_sends2:
            copy.wait_send()

    @pl.when(is3)
    def _():
        for copy in z_sends3:
            copy.wait_send()

    def drain(k):
        for dx in (1, 3):
            wait_bytes(sep.at[k, x], b_ssem.at[k, dx - 1])
            wait_bytes(sep.at[k, x, pl.ds(0, 128)], h_ssem.at[k, dx // 2])
        for f in range(4):
            wait_bytes(sep.at[k, f], f_ssem.at[k, f])

    @pl.when(c == 0)
    def _():
        drain(0)

    @pl.when(c == 1)
    def _():
        drain(1)
        drain(2)


def local(
    resid, rec_owner, rec_cell, leaf_inverse, couple_up, sep_inverse, couple_down, forward_field
):
    vmem = pl.BlockSpec(memory_space=pltpu.VMEM)
    hbm = pl.BlockSpec(memory_space=pl.ANY)
    V = pltpu.VMEM
    out = pl.pallas_call(
        kernel,
        out_shape=jax.ShapeDtypeStruct((1, 128), F32),
        in_specs=[hbm] * 8,
        out_specs=vmem,
        scratch_shapes=[
            V((8, 128), I32), V((8, 128), I32), V((1024, 128), F32), V((256, 1024), BF16),
            V((2, 128, 512), F32), V((3, 2, 1024, 128), F32),
            V((2, 256, 1024), F32), V((3, 2, 128, 1024), F32), V((128, 128), F32),
            V((256, 1024), BF16),
            V((3, 1024, 256), BF16), V((3, 1024, 256), BF16),
            V((4, 512, 512), BF16), V((3, 4, 256, 512), BF16),
            V((2, 4, 2, 128, 128), F32), V((2, 32, 32, 128), F32),
            V((16, 1, 128), F32), V((2, 32, 1, 128), F32),
            V((128, 512), F32), V((2, 4, 16, 512), F32), V((128, 512), F32),
            V((3, 512, 128), F32), V((3, 512, 128), F32), V((3, 512, 128), F32),
            V((4, 128, 128), F32), V((8, 64, 128), F32), V((16, 32, 128), F32),
            V((128, 128), F32), V((64, 128), F32), V((32, 128), F32),
            V((1024, 128), F32), V((3, 4, 256, 128), F32), V((128, 128), F32), V((128, 128), F32),
            DMA((8,)), DMA((2,)), DMA((2, 4)), DMA((2,)), DMA((2, 4)), DMA((2,)), DMA((2,)), DMA((2, 3)), DMA((2, 3)),
            DMA((3,)), DMA((3,)), DMA((3,)), DMA((3,)), DMA((3, 4)), DMA((4,)),
            DMA((3,)), DMA((3, 3)), DMA((3, 2)), DMA((3, 4)), DMA((3, 4)),
        ],
        compiler_params=pltpu.CompilerParams(
            collective_id=0, has_side_effects=True, vmem_limit_bytes=62 * 1024 * 1024
        ),
        name="adjoint_gradient",
    )(
        resid, rec_owner.reshape(8, 128), rec_cell.reshape(8, 128), leaf_inverse[0], couple_up[0],
        sep_inverse[0], couple_down[0], forward_field,
    )
    return out.reshape(128)


def solution(mesh):
    placed = (
        P(("leaf", "front"), None),
        P(("leaf", "front"), None),
        P(("leaf", "front")),
        P("leaf", None, "front", None),
        P("leaf", None, None, None, "front"),
        P("leaf", None, "front", None),
        P("leaf", None, None, "front", None),
        P(("leaf", "front"), None),
    )
    return jax.shard_map(
        local, mesh=mesh, in_specs=placed, out_specs=P(("leaf", "front")), check_vma=False
    )
```
